32 devices in a mesh: ka: 16 (over z, y, core), band: 2 (over x).
Axes of the slice: x: 2, y: 2, z: 4, core: 2. Of those that a mesh axis runs over, the one named last changes fastest.
Arguments:
- coefficients: bfloat16 [16, 2, 40, 2400], P('ka'), may hold values from -6 to 6
- class_weight: float32 [16], replicated, may hold values from 0.5 to 5
- diff_class: int32 [16, 16], replicated, may hold values from 0 to 15
- frag_cells: int32 [2], replicated, may hold values from 0 to 15
- block_pattern: int32 [2, 30], replicated, may hold values 0 or 1
Outputs:
- cluster: float32 [2, 2, 40, 2400], P(None, None, 'band', 'ka')
The draws below stay inside these ranges and needn't reach their ends.
All inputs are finite; a program needn't handle non-finite values.
Results may differ from the reference program's by a relative error of at most 0.0017.
Values may be sent and summed in bfloat16 or wider, within the bound.
A program may use at most 64 MiB of HBM per device.

```python
import math
import jax
import jax.numpy as jnp
from jax import lax

NAO = 2400
NBLK = 30
NFRAG = 2
NK = 16
NOCC = 40
BLK = 80


def set_ends(drawn, own_key, least, largest):
    shape = drawn.shape
    spot = [jax.random.randint(jax.random.fold_in(own_key, axis), (), 0, shape[axis]) for axis in range(len(shape))]
    drawn = drawn.at[tuple(spot)].set(least)
    longest = shape.index(max(shape))
    spot[longest] = (spot[longest] + 1) % shape[longest]
    return drawn.at[tuple(spot)].set(largest)


def levels(own_key, dims, split, low, top_value):
    loudness, own = 1.0, jax.random.fold_in(own_key, 6)
    for dim, parts in split:
        draws = jnp.exp(jax.random.uniform(jax.random.fold_in(own, dim), (parts,), jnp.float32, low / len(split), top_value / len(split)))
        loudness = loudness * jnp.repeat(draws, dims[dim] // parts).reshape([-1 if axis == dim else 1 for axis in range(len(dims))])
    return loudness


def normal_values(own_key, shape, scale, reach, split=(), held_as=jnp.bfloat16):
    array = jax.random.normal(own_key, shape, jnp.float32) * scale
    if len(split) > 0:
        array = levels(own_key, shape, split, -0.22, 0.18) * array
    return jnp.clip(array, min=-reach, max=reach).astype(held_as)


def setup_inputs(seed: int = 0) -> dict:
    arg_keys = jax.random.split(jax.random.key(seed), 6)
    return {
        "coefficients": normal_values(arg_keys[0], (NK, 2, NOCC, NAO), 1.0, 6.0, ((0, 16),)),
        "class_weight": jnp.clip(jnp.exp(jax.random.uniform(arg_keys[1], (NK,), jnp.float32, math.log(0.5), math.log(5.0))), 0.5, 5.0),
        "diff_class": set_ends(jax.random.randint(arg_keys[2], (NK, NK), 0, NK), jax.random.fold_in(arg_keys[2], 1), 0, NK - 1).astype(jnp.int32),
        "frag_cells": jax.random.randint(arg_keys[3], (NFRAG,), 0, NK).astype(jnp.int32),
        "block_pattern": set_ends((jax.random.randint(arg_keys[4], (NFRAG, NBLK), 0, 2) < 1).astype(jnp.int32), jax.random.fold_in(arg_keys[4], 1), 0, 1),
    }


def reference(coefficients, class_weight, diff_class, frag_cells, block_pattern):
    flat_coeff = coefficients.astype(jnp.float32).reshape(NK, 2 * NOCC, NAO)
    pair_weight = class_weight[diff_class]

    def step(running, kpoint):
        coeff_q = lax.dynamic_index_in_dim(flat_coeff, kpoint, 0, keepdims=False)
        intersection = jnp.einsum("ia,kja->kij", coeff_q, flat_coeff)
        m_real = intersection[:, :NOCC, :NOCC] + intersection[:, NOCC:, NOCC:]
        m_imag = intersection[:, :NOCC, NOCC:] - intersection[:, NOCC:, :NOCC]
        scaling = (lax.dynamic_index_in_dim(pair_weight, kpoint, 1, keepdims=False) / NAO)[:, None, None]
        m_real = lax.optimization_barrier((scaling * m_real).astype(jnp.bfloat16)).astype(jnp.float32)
        m_imag = lax.optimization_barrier((scaling * m_imag).astype(jnp.bfloat16)).astype(jnp.float32)
        m_block = jnp.concatenate([jnp.concatenate([m_real, m_imag], 2), jnp.concatenate([-m_imag, m_real], 2)], 1)
        return running + jnp.einsum("kio,ia->koa", m_block, coeff_q), None

    start_value = jnp.zeros((NK, 2 * NOCC, NAO), jnp.float32)
    exchange, _ = lax.scan(step, start_value, jnp.arange(NK, dtype=jnp.int32))
    w_real = exchange[:, :NOCC]
    w_imag = exchange[:, NOCC:]
    kpoints = jnp.arange(NK, dtype=jnp.int32)
    phase_index = (kpoints[None, :] * frag_cells[:, None]) % NK
    angles = 2.0 * jnp.pi * phase_index.astype(jnp.float32) / NK
    cosines = jnp.cos(angles) / NK
    sines = jnp.sin(angles) / NK
    high = lax.Precision.HIGHEST
    x_real = jnp.einsum("fk,kja->fja", cosines, w_real, precision=high) - jnp.einsum("fk,kja->fja", sines, w_imag, precision=high)
    x_imag = jnp.einsum("fk,kja->fja", sines, w_real, precision=high) + jnp.einsum("fk,kja->fja", cosines, w_imag, precision=high)
    block_ids = jnp.arange(NAO, dtype=jnp.int32) // BLK
    block_mask = block_pattern[:, block_ids].astype(jnp.float32)
    return jnp.stack([x_real, x_imag], 1) * block_mask[:, None, None, :]
```

```python
import functools
import math

import jax
import jax.numpy as jnp
from jax import lax
from jax.experimental import pallas as pl
from jax.experimental.pallas import tpu as pltpu
from jax.sharding import PartitionSpec as P

MESH = pl.DeviceIdType.MESH
LANES = 128
ROWS = 24
PAIR = 2 * ROWS
STRIDE = 32
SLOT = 64


def kernel(nk, bands, width, occupied, functions, blocks, cells,
           own, weight, classes, frag, pattern, out,
           sel, slots, stack, acc, acc_in, packed, part, part_in,
           right_s, right_r, left_s, left_r, win_s, win_r, gat_s, gat_r, one_s, one_r):
    n = nk // 2
    half = n // 2
    ka, band = lax.axis_index("ka"), lax.axis_index("band")
    chip, core = ka // 2, ka % 2
    padded = slots.shape[2]
    tiles = padded // LANES
    first = (tiles + 1) // 2 * LANES
    chunks = (pl.ds(0, first), pl.ds(first, padded - first))
    window = stack.shape[3]
    columns = functions // nk
    lanes = 2 * bands * STRIDE

    def chip_at(ring):
        return jnp.where(ring < half, 2 * ring, 2 * (n - 1 - ring) + 1)

    row, odd = chip // 2, chip % 2
    ring = jnp.where(odd == 0, row, n - 1 - row)

    def member(offset):
        return 2 * chip_at((ring + offset + n) % n) + core

    sibling = 2 * chip + 1 - core
    barrier = pltpu.get_barrier_semaphore()
    for offset in range(1, n):
        pl.semaphore_signal(barrier, inc=1, device_id=(member(offset), band), device_id_type=MESH)
    pl.semaphore_signal(barrier, inc=1, device_id=(sibling, band), device_id_type=MESH)
    for offset in range(1, bands):
        pl.semaphore_signal(barrier, inc=1, device_id=(ka, (band + offset) % bands), device_id_type=MESH)

    def pick(rows, target):
        r = lax.broadcasted_iota(jnp.int32, (rows, occupied), 0)
        c = lax.broadcasted_iota(jnp.int32, (rows, occupied), 1)
        return target(r, c).astype(jnp.bfloat16)

    def dot(a, b):
        return jnp.dot(a, b, preferred_element_type=jnp.float32)

    re, im = own[0, 0], own[0, 1]
    pick_re = pick(PAIR, lambda r, c: jnp.where((r < width) & (c == r + band * width), 1.0, 0.0))
    pick_im = pick(PAIR, lambda r, c: jnp.where(
        (r >= ROWS) & (r < ROWS + width) & (c == r - ROWS + band * width), 1.0, 0.0))
    slots[0, :, padded - LANES:] = jnp.zeros((PAIR, LANES), jnp.bfloat16)
    slots[0, :, :functions] = (dot(pick_re, re) + dot(pick_im, im)).astype(jnp.bfloat16)

    def group_pick(r, c):
        hit = jnp.zeros(r.shape, jnp.float32)
        for g in range(bands):
            low = ((band - g + bands) % bands) * width
            inside = (r >= g * STRIDE) & (r < g * STRIDE + width)
            hit = jnp.where(inside & (c - low == r - g * STRIDE), 1.0, hit)
        return hit

    pl.semaphore_wait(barrier, n - 1 + 1 + bands - 1)

    def ring_copy(to_right, s, h):
        if to_right:
            src, dst, ss, rs, to = s - 1, s, right_s, right_r, member(1)
        else:
            src, dst, ss, rs, to = (n - s + 1) % n, n - s, left_s, left_r, member(-1)
        return pltpu.make_async_remote_copy(
            src_ref=slots.at[src, :, chunks[h]], dst_ref=slots.at[dst, :, chunks[h]],
            send_sem=ss.at[s - 1, h], recv_sem=rs.at[s - 1, h],
            device_id=(to, band), device_id_type=MESH)

    def has(to_right, s, h):
        return s < half or (s == half and h == (0 if to_right else 1))

    start = pl.multiple_of(jnp.minimum(chip * 2 * columns // LANES, tiles - window // LANES) * LANES, LANES)

    def window_copy(g, t):
        return pltpu.make_async_remote_copy(
            src_ref=slots.at[t, :, pl.ds(start, window)], dst_ref=stack.at[t, g, pl.ds(0, PAIR), :],
            send_sem=win_s.at[g - 1, t], recv_sem=win_r.at[g - 1, t],
            device_id=(ka, (band + g) % bands), device_id_type=MESH)

    def spread(t):
        for g in range(1, bands):
            window_copy(g, t).start()
        stack[t, 0, 0:PAIR, :] = slots[t, :, pl.ds(start, window)]

    for h in range(2):
        for side in (True, False):
            if has(side, 1, h):
                ring_copy(side, 1, h).start()

    groups = pick(bands * STRIDE, group_pick)
    for ri, value in enumerate((re, im)):
        sel[core, ri, :, padded - LANES:] = jnp.zeros((bands * STRIDE, LANES), jnp.bfloat16)
        sel[core, ri, :, :functions] = dot(groups, value).astype(jnp.bfloat16)
    sel_copy = pltpu.make_async_remote_copy(
        src_ref=sel.at[core], dst_ref=sel.at[core], send_sem=one_s.at[0], recv_sem=one_r.at[0],
        device_id=(sibling, band), device_id_type=MESH)
    sel_copy.start()
    stack[:, :, PAIR:, :] = jnp.zeros((n, bands, SLOT - PAIR, window), jnp.bfloat16)
    spread(0)

    at = lax.broadcasted_iota(jnp.int32, (n, lanes), 0)
    where = ring - at
    where = jnp.where(where < 0, where + n, where)
    kpoint = (2 * chip_at(where) + core).astype(jnp.float32)
    cosines, sines = [], []
    for f in range(cells):
        turns = kpoint * (frag[f].astype(jnp.float32) / nk)
        angle = 2.0 * math.pi * (turns - jnp.floor(turns))
        cosines.append(jnp.cos(angle) / nk)
        sines.append(jnp.sin(angle) / nk)
    wide = (columns + LANES - 1) // LANES * LANES
    column = lax.broadcasted_iota(jnp.int32, (ROWS, wide), 1) + ka * columns
    block = functions // blocks
    masks = []
    for f in range(cells):
        mask = jnp.zeros((ROWS, wide), jnp.float32)
        for i in range(blocks):
            keep = (column >= i * block) & (column < (i + 1) * block)
            mask = jnp.where(keep, pattern[f, i].astype(jnp.float32), mask)
        masks.append(mask)

    lane = lax.broadcasted_iota(jnp.int32, (ROWS, lanes), 1)
    lane_core = lane // (lanes // 2)

    def overlap(t):
        k = member(-t)
        block_k = slots[t]
        pieces = []
        for ri in range(2):
            cols = [lax.dot_general(block_k, sel[c, ri], (((1,), (1,)), ((), ())),
                                    preferred_element_type=jnp.float32) for c in range(2)]
            pieces.append(jnp.concatenate(cols, 1))
        by_re, by_im = pieces
        m_real = by_re[:ROWS] + by_im[ROWS:]
        m_imag = by_re[ROWS:] - by_im[:ROWS]
        scale = jnp.where(lane_core == 0, weight[classes[k, 2 * chip]], weight[classes[k, 2 * chip + 1]])
        scale = scale / functions
        m_real = (scale * m_real).astype(jnp.bfloat16).astype(jnp.float32)
        m_imag = (scale * m_imag).astype(jnp.bfloat16).astype(jnp.float32)
        for f in range(cells):
            co, si = cosines[f][t:t + 1], sines[f][t:t + 1]
            a, b = co * m_real - si * m_imag, si * m_real + co * m_imag
            for ri, value in enumerate((a, b)):
                spot = pl.ds((2 * f + ri) * ROWS, ROWS)
                if t == 0:
                    acc[spot, :] = value
                else:
                    acc[spot, :] += value

    sel_copy.wait()
    overlap(0)
    for s in range(1, half + 1):
        for h in range(2):
            for side in (True, False):
                if has(side, s, h):
                    ring_copy(side, s, h).wait_recv()
                    if has(side, s + 1, h):
                        ring_copy(side, s + 1, h).start()
        spread(s)
        if s < half:
            spread(n - s)
        overlap(s)
        if s < half:
            overlap(n - s)

    acc_copy = pltpu.make_async_remote_copy(
        src_ref=acc, dst_ref=acc_in, send_sem=one_s.at[1], recv_sem=one_r.at[1],
        device_id=(sibling, band), device_id_type=MESH)
    acc_copy.start()
    acc_copy.wait_recv()
    total = acc[...] + acc_in[...]
    total = jnp.where(core == 0, total, pltpu.roll(total, lanes // 2, 1))
    for f in range(cells):
        n_re = total[2 * f * ROWS:(2 * f + 1) * ROWS]
        n_im = total[(2 * f + 1) * ROWS:(2 * f + 2) * ROWS]
        value = jnp.zeros((ROWS, lanes), jnp.float32)
        for g in range(bands):
            low = g * SLOT
            a = n_re if g == 0 else pltpu.roll(n_re, g * (SLOT - STRIDE), 1)
            b = pltpu.roll(n_im, g * (SLOT - STRIDE) + ROWS, 1)
            value = jnp.where((lane >= low) & (lane < low + ROWS), a, value)
            value = jnp.where((lane >= low + ROWS) & (lane < low + PAIR), -b, value)
        packed[0, f * ROWS:(f + 1) * ROWS, :] = value

    def gather_copy(t):
        return pltpu.make_async_remote_copy(
            src_ref=packed.at[0], dst_ref=packed.at[t], send_sem=gat_s.at[t - 1], recv_sem=gat_r.at[t - 1],
            device_id=(member(t), band), device_id_type=MESH)

    order = sorted(range(1, n), key=lambda t: -min(t, n - t))
    for t in order:
        gather_copy(t).start()
    for g in range(1, bands):
        for t in range(n):
            window_copy(g, t).wait_recv()
    for t in order:
        gather_copy(t).wait_recv()

    spot = lane % SLOT
    left = []
    for f in range(cells):
        real, imag = [], []
        for t in range(n):
            x = packed[t, f * ROWS:(f + 1) * ROWS, :]
            real.append(x)
            y = jnp.where(spot < ROWS, -pltpu.roll(x, lanes - ROWS, 1), pltpu.roll(x, ROWS, 1))
            imag.append(jnp.where(spot < PAIR, y, 0.0))
        left += [jnp.concatenate(real, 1), jnp.concatenate(imag, 1)]
    left = jnp.concatenate(left, 0)
    high = left.astype(jnp.bfloat16)
    low = (left - high.astype(jnp.float32)).astype(jnp.bfloat16)
    terms = stack[...].reshape(n * bands * SLOT, window)
    result = dot(high, terms) + dot(low, terms)
    offset = chip * 2 * columns - start

    def cut(c):
        return pltpu.roll(result, window - offset - c * columns, 1)[:, :wide]

    part[...] = cut(1 - core)
    part_copy = pltpu.make_async_remote_copy(
        src_ref=part, dst_ref=part_in, send_sem=one_s.at[2], recv_sem=one_r.at[2],
        device_id=(sibling, band), device_id_type=MESH)
    part_copy.start()
    mine = cut(core)
    part_copy.wait_recv()
    whole = mine + part_in[...]
    for f in range(cells):
        for ri in range(2):
            low_row = (2 * f + ri) * ROWS
            value = whole[low_row:low_row + ROWS] * masks[f]
            out[f, ri] = value[:width, :columns]

    for s in range(1, half + 1):
        for h in range(2):
            for side in (True, False):
                if has(side, s, h):
                    ring_copy(side, s, h).wait_send()
    for g in range(1, bands):
        for t in range(n):
            window_copy(g, t).wait_send()
    for t in order:
        gather_copy(t).wait_send()
    acc_copy.wait_send()
    part_copy.wait_send()


def solution(mesh):
    nk, bands = mesh.shape["ka"], mesh.shape["band"]
    n = nk // 2

    def shards(coefficients, class_weight, diff_class, frag_cells, block_pattern):
        occupied, functions = coefficients.shape[2:]
        width = occupied // bands
        cells, blocks = block_pattern.shape
        padded = (functions + LANES - 1) // LANES * LANES
        columns = functions // nk
        window = (2 * columns + 2 * LANES - 2) // LANES * LANES
        wide = (columns + LANES - 1) // LANES * LANES
        lanes = 2 * bands * STRIDE
        rows = 2 * cells * ROWS
        vmem, smem = pl.BlockSpec(memory_space=pltpu.VMEM), pl.BlockSpec(memory_space=pltpu.SMEM)
        bf16, f32 = jnp.bfloat16, jnp.float32
        dma = pltpu.SemaphoreType.DMA
        return pl.pallas_call(
            functools.partial(kernel, nk, bands, width, occupied, functions, blocks, cells),
            out_shape=jax.ShapeDtypeStruct((cells, 2, width, columns), f32),
            in_specs=[vmem, smem, smem, smem, smem],
            out_specs=vmem,
            scratch_shapes=[
                pltpu.VMEM((2, 2, bands * STRIDE, padded), bf16),
                pltpu.VMEM((n, PAIR, padded), bf16),
                pltpu.VMEM((n, bands, SLOT, window), bf16),
                pltpu.VMEM((rows, lanes), f32),
                pltpu.VMEM((rows, lanes), f32),
                pltpu.VMEM((n, cells * ROWS, lanes), f32),
                pltpu.VMEM((rows, wide), f32),
                pltpu.VMEM((rows, wide), f32),
                dma((n // 2, 2)), dma((n // 2, 2)), dma((n // 2, 2)), dma((n // 2, 2)),
                dma((bands - 1, n)), dma((bands - 1, n)),
                dma((n - 1,)), dma((n - 1,)), dma((3,)), dma((3,)),
            ],
            compiler_params=pltpu.CompilerParams(
                collective_id=0, has_side_effects=True, vmem_limit_bytes=52 * 2**20),
            cost_estimate=pl.CostEstimate(
                flops=2 * n * PAIR * 2 * lanes * padded, bytes_accessed=4 * n * PAIR * padded, transcendentals=0),
            name="exchange",
        )(coefficients, class_weight, diff_class, frag_cells, block_pattern)

    placed = (P("ka", None, None, None), P(), P(), P(), P())
    return jax.shard_map(
        shards, mesh=mesh, in_specs=placed, out_specs=P(None, None, "band", "ka"), check_vma=False)
```

```python
import functools
import math

import jax
import jax.numpy as jnp
from jax import lax
from jax.experimental import pallas as pl
from jax.experimental.pallas import tpu as pltpu
from jax.sharding import PartitionSpec as P

MESH = pl.DeviceIdType.MESH
LANES = 128
STRIDE = 32


def kernel(nk, bands, width, occupied, functions, blocks, cells,
           own_hbm, weight_hbm, classes_hbm, frag_hbm, pattern_hbm, out,
           own, weight, classes, frag, pattern,
           sel, slots, near, stack, acc, acc_in, packed, part, part_in,
           in_s, right_s, right_r, left_s, left_r, win_s, win_r, gat_s, gat_r, one_s, one_r):
    n = nk // 2
    half = n // 2
    ka, band = lax.axis_index("ka"), lax.axis_index("band")
    chip, core = ka // 2, ka % 2
    padded = slots.shape[2]
    tiles = padded // LANES
    first = (tiles + 1) // 2 * LANES
    chunks = (pl.ds(0, first), pl.ds(first, padded - first))
    window = stack.shape[2]
    columns = functions // nk
    lanes = 2 * bands * STRIDE
    rows = cells * width
    f32, bf16 = jnp.float32, jnp.bfloat16

    operands = (own_hbm, weight_hbm, classes_hbm, frag_hbm, pattern_hbm)
    fetches = [pltpu.make_async_copy(src, dst, in_s.at[i])
               for i, (src, dst) in enumerate(zip(operands, (own, weight, classes, frag, pattern)))]
    for fetch in fetches:
        fetch.start()

    def chip_at(ring):
        return jnp.where(ring < half, 2 * ring, 2 * (n - 1 - ring) + 1)

    row, odd = chip // 2, chip % 2
    ring = jnp.where(odd == 0, row, n - 1 - row)

    def member(offset):
        return 2 * chip_at((ring + offset + n) % n) + core

    sibling = 2 * chip + 1 - core
    barrier = pltpu.get_barrier_semaphore()
    for offset in range(1, n):
        pl.semaphore_signal(barrier, inc=1, device_id=(member(offset), band), device_id_type=MESH)
    pl.semaphore_signal(barrier, inc=1, device_id=(sibling, band), device_id_type=MESH)
    for offset in range(1, bands):
        pl.semaphore_signal(barrier, inc=1, device_id=(ka, (band + offset) % bands), device_id_type=MESH)

    def dot(a, b):
        return jnp.dot(a, b, preferred_element_type=f32)

    def iotas(shape):
        return (lax.broadcasted_iota(jnp.int32, shape, 0), lax.broadcasted_iota(jnp.int32, shape, 1))

    slots[0, :, padded - LANES:] = jnp.zeros((2 * width, LANES), bf16)
    r, c = iotas((2 * width, occupied))
    c = c - band * width
    pick_re = jnp.where((c >= 0) & (c < width) & (c == r), 1.0, 0.0).astype(bf16)
    pick_im = jnp.where((c >= 0) & (c < width) & (c == r - width), 1.0, 0.0).astype(bf16)
    fetches[0].wait()
    re, im = own[0, 0], own[0, 1]
    slots[0, :, :functions] = (dot(pick_re, re) + dot(pick_im, im)).astype(bf16)

    pl.semaphore_wait(barrier, n - 1 + 1 + bands - 1)

    def ring_copy(to_right, s, h):
        if to_right:
            src, dst, ss, rs, to = s - 1, s, right_s, right_r, member(1)
        else:
            src, dst, ss, rs, to = (n - s + 1) % n, n - s, left_s, left_r, member(-1)
        return pltpu.make_async_remote_copy(
            src_ref=slots.at[src, :, chunks[h]], dst_ref=slots.at[dst, :, chunks[h]],
            send_sem=ss.at[s - 1, h], recv_sem=rs.at[s - 1, h],
            device_id=(to, band), device_id_type=MESH)

    def has(to_right, s, h):
        return s < half or (s == half and h == (0 if to_right else 1))

    start = pl.multiple_of(jnp.minimum(chip * 2 * columns // LANES, tiles - window // LANES) * LANES, LANES)

    def window_copy(g, t):
        return pltpu.make_async_remote_copy(
            src_ref=slots.at[t, :, pl.ds(start, window)], dst_ref=near.at[g - 1, t],
            send_sem=win_s.at[g - 1, t], recv_sem=win_r.at[g - 1, t],
            device_id=(ka, (band + g) % bands), device_id_type=MESH)

    def spread(t):
        for g in range(1, bands):
            window_copy(g, t).start()

    for h in range(2):
        for side in (True, False):
            if has(side, 1, h):
                ring_copy(side, 1, h).start()
    spread(0)

    r, c = iotas((occupied, lanes))
    hits = [jnp.zeros(r.shape, f32), jnp.zeros(r.shape, f32)]
    for ri in range(2):
        for g in range(bands):
            low = (ri * bands + g) * STRIDE
            inside = (c >= low) & (c < low + width)
            hits[ri] = jnp.where(inside & (r - ((band - g + bands) % bands) * width == c - low), 1.0, hits[ri])
    mine = pl.ds(pl.multiple_of(core * lanes, LANES), lanes)
    sel[padded - LANES:, mine] = jnp.zeros((LANES, lanes), bf16)

    def turned(value, hit):
        return lax.dot_general(value, hit.astype(bf16), (((0,), (0,)), ((), ())), preferred_element_type=f32)

    sel[:functions, mine] = (turned(re, hits[0]) + turned(im, hits[1])).astype(bf16)
    sel_copy = pltpu.make_async_remote_copy(
        src_ref=sel.at[:, mine], dst_ref=sel.at[:, mine], send_sem=one_s.at[0], recv_sem=one_r.at[0],
        device_id=(sibling, band), device_id_type=MESH)
    sel_copy.start()
    for fetch in fetches[1:]:
        fetch.wait()

    at = lax.broadcasted_iota(jnp.int32, (n, 2 * lanes), 0)
    where = ring - at
    where = jnp.where(where < 0, where + n, where)
    kpoint = (2 * chip_at(where) + core).astype(f32)
    lane = lax.broadcasted_iota(jnp.int32, (n, 2 * lanes), 1)
    sign = jnp.where(lane % lanes < lanes // 2, 1.0, -1.0)
    cosines, sines = [], []
    for f in range(cells):
        turns = kpoint * (frag[f].astype(f32) / nk)
        angle = 2.0 * math.pi * (turns - jnp.floor(turns))
        cosines.append(jnp.cos(angle) / nk)
        sines.append(sign * jnp.sin(angle) / nk)
    wide = (columns + LANES - 1) // LANES * LANES
    column = lax.broadcasted_iota(jnp.int32, (width, wide), 1) + ka * columns
    block = functions // blocks
    masks = []
    for f in range(cells):
        mask = jnp.zeros((width, wide), f32)
        for i in range(blocks):
            keep = (column >= i * block) & (column < (i + 1) * block)
            mask = jnp.where(keep, pattern[f, i].astype(f32), mask)
        masks.append(mask)

    def swap(x):
        return pltpu.roll(x, lanes // 2, 1)

    def swap_both(x):
        return jnp.concatenate([swap(x[:, :lanes]), swap(x[:, lanes:])], 1)

    own_lane = lax.broadcasted_iota(jnp.int32, (width, 2 * lanes), 1)
    signs = jnp.where(own_lane % lanes < lanes // 2, 1.0, -1.0)

    def overlap(t):
        k = member(-t)
        product = dot(slots[t], sel[...])
        value = product[:width] + signs * swap_both(product[width:])
        scale = jnp.where(own_lane < lanes, weight[classes[k, 2 * chip]], weight[classes[k, 2 * chip + 1]])
        value = (scale / functions * value).astype(bf16).astype(f32)
        other = swap_both(value)
        terms = jnp.concatenate(
            [cosines[f][t:t + 1] * value + sines[f][t:t + 1] * other for f in range(cells)], 0)
        if t == 0:
            acc[...] = terms
        else:
            acc[...] += terms

    r, c = iotas((lanes, 2 * width))
    placers = []
    for g in range(bands):
        a, b = g * STRIDE, (bands + g) * STRIDE
        hit = ((c < width) & (r == a + c)) | ((c >= width) & (r == b + c - width))
        placers.append(jnp.where(hit, 1.0, 0.0).astype(bf16))

    def place(t):
        value = dot(placers[0], slots[t, :, pl.ds(start, window)])
        for g in range(1, bands):
            window_copy(g, t).wait_recv()
            value = value + dot(placers[g], near[g - 1, t])
        stack[t] = value.astype(bf16)

    sel_copy.wait()
    for s in range(1, half + 1):
        before = [s - 1] if s == 1 else [s - 1, n - s + 1]
        for h in range(2):
            for side in (True, False):
                if has(side, s, h):
                    ring_copy(side, s, h).wait_recv()
                    if has(side, s + 1, h):
                        ring_copy(side, s + 1, h).start()
            if h == 0:
                overlap(before[0])
        spread(s)
        if s < half:
            spread(n - s)
        for t in before[1:]:
            overlap(t)
        if s < half:
            for t in before:
                place(t)
    overlap(half)

    acc_copy = pltpu.make_async_remote_copy(
        src_ref=acc, dst_ref=acc_in, send_sem=one_s.at[1], recv_sem=one_r.at[1],
        device_id=(sibling, band), device_id_type=MESH)
    acc_copy.start()
    acc_copy.wait_recv()
    packed[0] = acc[:, mine] + acc_in[:, mine]

    def gather_copy(t):
        return pltpu.make_async_remote_copy(
            src_ref=packed.at[0], dst_ref=packed.at[t], send_sem=gat_s.at[t - 1], recv_sem=gat_r.at[t - 1],
            device_id=(member(t), band), device_id_type=MESH)

    order = sorted(range(1, n), key=lambda t: -min(t, n - t))
    for t in order:
        gather_copy(t).start()
    for t in (half - 1, half + 1, half):
        place(t)
    for t in order:
        gather_copy(t).wait_recv()

    rotated = lax.broadcasted_iota(jnp.int32, (rows, lanes), 1)
    flip = jnp.where(rotated < lanes // 2, -1.0, 1.0)
    real = [packed[t] for t in range(n)]
    left = jnp.concatenate(
        [jnp.concatenate(real, 1), jnp.concatenate([flip * swap(x) for x in real], 1)], 0)
    high = left.astype(bf16)
    low = (left - high.astype(f32)).astype(bf16)
    terms = stack[...].reshape(n * lanes, window)
    result = dot(high, terms) + dot(low, terms)
    offset = chip * 2 * columns - start

    def cut(c):
        return pltpu.roll(result, window - offset - c * columns, 1)[:, :wide]

    part[...] = cut(1 - core)
    part_copy = pltpu.make_async_remote_copy(
        src_ref=part, dst_ref=part_in, send_sem=one_s.at[2], recv_sem=one_r.at[2],
        device_id=(sibling, band), device_id_type=MESH)
    part_copy.start()
    kept = cut(core)
    part_copy.wait_recv()
    whole = kept + part_in[...]
    for ri in range(2):
        for f in range(cells):
            spot = (ri * cells + f) * width
            out[f, ri] = (whole[spot:spot + width] * masks[f])[:, :columns]

    for s in range(1, half + 1):
        for h in range(2):
            for side in (True, False):
                if has(side, s, h):
                    ring_copy(side, s, h).wait_send()
    for g in range(1, bands):
        for t in range(n):
            window_copy(g, t).wait_send()
    for t in order:
        gather_copy(t).wait_send()
    acc_copy.wait_send()
    part_copy.wait_send()


def solution(mesh):
    nk, bands = mesh.shape["ka"], mesh.shape["band"]
    n = nk // 2

    def shards(coefficients, class_weight, diff_class, frag_cells, block_pattern):
        occupied, functions = coefficients.shape[2:]
        width = occupied // bands
        cells, blocks = block_pattern.shape
        padded = (functions + LANES - 1) // LANES * LANES
        columns = functions // nk
        window = (2 * columns + 2 * LANES - 2) // LANES * LANES
        wide = (columns + LANES - 1) // LANES * LANES
        lanes = 2 * bands * STRIDE
        rows = cells * width
        hbm = pl.BlockSpec(memory_space=pl.ANY)
        bf16, f32 = jnp.bfloat16, jnp.float32
        dma = pltpu.SemaphoreType.DMA
        operands = (coefficients, class_weight, diff_class, frag_cells, block_pattern)
        return pl.pallas_call(
            functools.partial(kernel, nk, bands, width, occupied, functions, blocks, cells),
            out_shape=jax.ShapeDtypeStruct((cells, 2, width, columns), f32),
            in_specs=[hbm] * 5,
            out_specs=pl.BlockSpec(memory_space=pltpu.VMEM),
            scratch_shapes=[
                pltpu.VMEM(coefficients.shape, bf16),
                *[pltpu.SMEM(x.shape, x.dtype) for x in operands[1:]],
                pltpu.VMEM((padded, 2 * lanes), bf16),
                pltpu.VMEM((n, 2 * width, padded), bf16),
                pltpu.VMEM((bands - 1, n, 2 * width, window), bf16),
                pltpu.VMEM((n, lanes, window), bf16),
                pltpu.VMEM((rows, 2 * lanes), f32),
                pltpu.VMEM((rows, 2 * lanes), f32),
                pltpu.VMEM((n, rows, lanes), f32),
                pltpu.VMEM((2 * rows, wide), f32),
                pltpu.VMEM((2 * rows, wide), f32),
                dma((5,)),
                dma((n // 2, 2)), dma((n // 2, 2)), dma((n // 2, 2)), dma((n // 2, 2)),
                dma((bands - 1, n)), dma((bands - 1, n)),
                dma((n - 1,)), dma((n - 1,)), dma((3,)), dma((3,)),
            ],
            compiler_params=pltpu.CompilerParams(
                collective_id=0, has_side_effects=True, vmem_limit_bytes=52 * 2**20),
            cost_estimate=pl.CostEstimate(
                flops=8 * n * width * lanes * padded, bytes_accessed=8 * n * width * padded, transcendentals=0),
            name="exchange",
        )(*operands)

    placed = (P("ka", None, None, None), P(), P(), P(), P())
    return jax.shard_map(
        shards, mesh=mesh, in_specs=placed, out_specs=P(None, None, "band", "ka"), check_vma=False)
```

```python
import functools
import math

import jax
import jax.numpy as jnp
from jax import lax
from jax.experimental import pallas as pl
from jax.experimental.pallas import tpu as pltpu
from jax.sharding import PartitionSpec as P

MESH = pl.DeviceIdType.MESH
LANES = 128
STRIDE = 32


def kernel(nk, bands, width, occupied, functions, blocks, cells,
           own_hbm, weight_hbm, classes_hbm, frag_hbm, pattern_hbm, out,
           own, weight, classes, frag, pattern,
           sel, slots, near, stack, turn, acc, acc_in, packed, part, part_in,
           in_s, right_s, right_r, left_s, left_r, win_s, win_r, gat_s, gat_r, one_s, one_r):
    n = nk // 2
    half = n // 2
    ka, band = lax.axis_index("ka"), lax.axis_index("band")
    chip, core = ka // 2, ka % 2
    padded = slots.shape[2]
    tiles = padded // LANES
    first = (tiles + 1) // 2 * LANES
    chunks = (pl.ds(0, first), pl.ds(first, padded - first))
    window = stack.shape[2]
    columns = functions // nk
    lanes = 2 * bands * STRIDE
    rows = cells * width
    f32, bf16 = jnp.float32, jnp.bfloat16

    operands = (own_hbm, weight_hbm, classes_hbm, frag_hbm, pattern_hbm)
    fetches = [pltpu.make_async_copy(src, dst, in_s.at[i])
               for i, (src, dst) in enumerate(zip(operands, (own, weight, classes, frag, pattern)))]
    for fetch in fetches:
        fetch.start()

    def chip_at(ring):
        return jnp.where(ring < half, 2 * ring, 2 * (n - 1 - ring) + 1)

    row, odd = chip // 2, chip % 2
    ring = jnp.where(odd == 0, row, n - 1 - row)

    def wrap(x):
        x = jnp.where(x >= n, x - n, x)
        return jnp.where(x < 0, x + n, x)

    members = [2 * chip_at(wrap(ring + offset)) + core for offset in range(n)]

    def member(offset):
        return members[offset % n]

    def place_of(t):
        return 2 * t - 1 if 0 < t <= half else 2 * ((n - t) % n)

    sibling = 2 * chip + 1 - core
    barrier = pltpu.get_barrier_semaphore()
    for offset in range(1, n):
        pl.semaphore_signal(barrier, inc=1, device_id=(member(offset), band), device_id_type=MESH)
    pl.semaphore_signal(barrier, inc=1, device_id=(sibling, band), device_id_type=MESH)
    for offset in range(1, bands):
        pl.semaphore_signal(barrier, inc=1, device_id=(ka, (band + offset) % bands), device_id_type=MESH)

    def dot(a, b):
        return jnp.dot(a, b, preferred_element_type=f32)

    def iotas(shape):
        return (lax.broadcasted_iota(jnp.int32, shape, 0), lax.broadcasted_iota(jnp.int32, shape, 1))

    slots[0, :, padded - LANES:] = jnp.zeros((2 * width, LANES), bf16)
    r, c = iotas((2 * width, occupied))
    c = c - band * width
    pick_re = jnp.where((c >= 0) & (c < width) & (c == r), 1.0, 0.0).astype(bf16)
    pick_im = jnp.where((c >= 0) & (c < width) & (c == r - width), 1.0, 0.0).astype(bf16)
    fetches[0].wait()
    re, im = own[0, 0], own[0, 1]
    slots[0, :, :functions] = (dot(pick_re, re) + dot(pick_im, im)).astype(bf16)

    pl.semaphore_wait(barrier, n - 1 + 1 + bands - 1)

    def ring_copy(to_right, s, h):
        if to_right:
            src, dst, ss, rs, to = jnp.maximum(2 * s - 3, 0), 2 * s - 1, right_s, right_r, member(1)
        else:
            dst = jnp.where(s == half, n - 1, 2 * s)
            src, ss, rs, to = 2 * s - 2, left_s, left_r, member(-1)
        return pltpu.make_async_remote_copy(
            src_ref=slots.at[src, :, chunks[h]], dst_ref=slots.at[dst, :, chunks[h]],
            send_sem=ss.at[s - 1, h], recv_sem=rs.at[s - 1, h],
            device_id=(to, band), device_id_type=MESH)

    def steps(to_right, h):
        return half if h == (0 if to_right else 1) else half - 1

    start = pl.multiple_of(jnp.minimum(chip * 2 * columns // LANES, tiles - window // LANES) * LANES, LANES)

    def window_copy(g, t):
        return pltpu.make_async_remote_copy(
            src_ref=slots.at[t, :, pl.ds(start, window)], dst_ref=near.at[g - 1, t],
            send_sem=win_s.at[g - 1, t], recv_sem=win_r.at[g - 1, t],
            device_id=(ka, (band + g) % bands), device_id_type=MESH)

    def spread(t):
        for g in range(1, bands):
            window_copy(g, t).start()

    for h in range(2):
        for side in (True, False):
            ring_copy(side, 1, h).start()
    spread(0)

    r, c = iotas((occupied, lanes))
    hits = [jnp.zeros(r.shape, f32), jnp.zeros(r.shape, f32)]
    for ri in range(2):
        for g in range(bands):
            low = (ri * bands + g) * STRIDE
            inside = (c >= low) & (c < low + width)
            hits[ri] = jnp.where(inside & (r - ((band - g + bands) % bands) * width == c - low), 1.0, hits[ri])
    mine = pl.ds(pl.multiple_of(core * lanes, LANES), lanes)
    sel[padded - LANES:, mine] = jnp.zeros((LANES, lanes), bf16)

    def turned(value, hit):
        return lax.dot_general(value, hit.astype(bf16), (((0,), (0,)), ((), ())), preferred_element_type=f32)

    sel[:functions, mine] = (turned(re, hits[0]) + turned(im, hits[1])).astype(bf16)
    sel_copy = pltpu.make_async_remote_copy(
        src_ref=sel.at[:, mine], dst_ref=sel.at[:, mine], send_sem=one_s.at[0], recv_sem=one_r.at[0],
        device_id=(sibling, band), device_id_type=MESH)
    sel_copy.start()
    for fetch in fetches[1:]:
        fetch.wait()

    at = lax.broadcasted_iota(jnp.int32, (n, 2 * lanes), 0)
    where = wrap(jnp.where(at % 2 == 0, ring + at // 2, ring - at // 2 - 1))
    kpoint = (2 * chip_at(where) + core).astype(f32)
    lane = lax.broadcasted_iota(jnp.int32, (n, 2 * lanes), 1)
    sign = jnp.where(lane % lanes < lanes // 2, 1.0, -1.0)
    for f in range(cells):
        turns = kpoint * (frag[f].astype(f32) / nk)
        angle = 2.0 * math.pi * (turns - jnp.floor(turns))
        turn[f] = jnp.cos(angle) / nk
        turn[cells + f] = sign * jnp.sin(angle) / nk
    wide = (columns + LANES - 1) // LANES * LANES
    column = lax.broadcasted_iota(jnp.int32, (width, wide), 1) + ka * columns
    block = functions // blocks
    masks = []
    for f in range(cells):
        mask = jnp.zeros((width, wide), f32)
        for i in range(blocks):
            keep = (column >= i * block) & (column < (i + 1) * block)
            mask = jnp.where(keep, pattern[f, i].astype(f32), mask)
        masks.append(mask)

    def swap(x):
        return pltpu.roll(x, lanes // 2, 1)

    def swap_both(x):
        return jnp.concatenate([swap(x[:, :lanes]), swap(x[:, lanes:])], 1)

    own_lane = lax.broadcasted_iota(jnp.int32, (width, 2 * lanes), 1)
    signs = jnp.where(own_lane % lanes < lanes // 2, 1.0, -1.0)

    def overlap(i):
        both = slots[pl.ds(2 * i, 2)].reshape(4 * width, padded)
        product = dot(both, sel[...])
        for side in range(2):
            low = 2 * width * side
            k = 2 * chip_at(wrap(ring - i - 1 if side else ring + i)) + core
            value = product[low:low + width] + signs * swap_both(product[low + width:low + 2 * width])
            scale = jnp.where(own_lane < lanes, weight[classes[k, 2 * chip]], weight[classes[k, 2 * chip + 1]])
            value = (scale / functions * value).astype(bf16).astype(f32)
            other = swap_both(value)
            at = pl.ds(2 * i + side, 1)
            acc[...] += jnp.concatenate(
                [turn[f, at, :] * value + turn[cells + f, at, :] * other for f in range(cells)], 0)

    r, c = iotas((lanes, 2 * width))
    placers = []
    for g in range(bands):
        a, b = g * STRIDE, (bands + g) * STRIDE
        hit = ((c < width) & (r == a + c)) | ((c >= width) & (r == b + c - width))
        placers.append(jnp.where(hit, 1.0, 0.0).astype(bf16))

    def place(t):
        value = dot(placers[0], slots[t, :, pl.ds(start, window)])
        for g in range(1, bands):
            window_copy(g, t).wait_recv()
            value = value + dot(placers[g], near[g - 1, t])
        stack[t] = value.astype(bf16)

    acc[...] = jnp.zeros((rows, 2 * lanes), f32)
    sel_copy.wait()

    @pl.loop(0, half)
    def _(i):
        s = i + 1
        for h in range(2):
            for side in (True, False):
                last = steps(side, h)

                @pl.when(s <= last)
                def _():
                    ring_copy(side, s, h).wait_recv()

                @pl.when(s < last)
                def _():
                    ring_copy(side, s + 1, h).start()
        spread(2 * s - 1)

        @pl.when(s < half)
        def _():
            spread(2 * s)

        overlap(i)

    acc_copy = pltpu.make_async_remote_copy(
        src_ref=acc, dst_ref=acc_in, send_sem=one_s.at[1], recv_sem=one_r.at[1],
        device_id=(sibling, band), device_id_type=MESH)
    acc_copy.start()
    acc_copy.wait_recv()
    packed[0] = acc[:, mine] + acc_in[:, mine]

    def gather_copy(t):
        return pltpu.make_async_remote_copy(
            src_ref=packed.at[0], dst_ref=packed.at[place_of(t)], send_sem=gat_s.at[t - 1], recv_sem=gat_r.at[t - 1],
            device_id=(member(t), band), device_id_type=MESH)

    order = sorted(range(1, n), key=lambda t: -min(t, n - t))
    for t in order:
        gather_copy(t).start()
    pl.loop(0, n)(place)
    for t in order:
        gather_copy(t).wait_recv()

    rotated = lax.broadcasted_iota(jnp.int32, (rows, lanes), 1)
    flip = jnp.where(rotated < lanes // 2, -1.0, 1.0)
    real = [packed[t] for t in range(n)]
    left = jnp.concatenate(
        [jnp.concatenate(real, 1), jnp.concatenate([flip * swap(x) for x in real], 1)], 0)
    high = left.astype(bf16)
    low = (left - high.astype(f32)).astype(bf16)
    terms = stack[...].reshape(n * lanes, window)
    result = dot(jnp.concatenate([high, low], 0), terms)
    result = result[:2 * rows] + result[2 * rows:]
    offset = chip * 2 * columns - start

    def cut(c):
        return pltpu.roll(result, window - offset - c * columns, 1)[:, :wide]

    part[...] = cut(1 - core)
    part_copy = pltpu.make_async_remote_copy(
        src_ref=part, dst_ref=part_in, send_sem=one_s.at[2], recv_sem=one_r.at[2],
        device_id=(sibling, band), device_id_type=MESH)
    part_copy.start()
    kept = cut(core)
    part_copy.wait_recv()
    whole = kept + part_in[...]
    for ri in range(2):
        for f in range(cells):
            spot = (ri * cells + f) * width
            out[f, ri] = (whole[spot:spot + width] * masks[f])[:, :columns]

    @pl.loop(1, half + 1)
    def _(s):
        for h in range(2):
            for side in (True, False):
                @pl.when(s <= steps(side, h))
                def _():
                    ring_copy(side, s, h).wait_send()

    @pl.loop(0, n)
    def _(t):
        for g in range(1, bands):
            window_copy(g, t).wait_send()

    for t in order:
        gather_copy(t).wait_send()
    acc_copy.wait_send()
    part_copy.wait_send()


def solution(mesh):
    nk, bands = mesh.shape["ka"], mesh.shape["band"]
    n = nk // 2

    def shards(coefficients, class_weight, diff_class, frag_cells, block_pattern):
        occupied, functions = coefficients.shape[2:]
        width = occupied // bands
        cells, blocks = block_pattern.shape
        padded = (functions + LANES - 1) // LANES * LANES
        columns = functions // nk
        window = (2 * columns + 2 * LANES - 2) // LANES * LANES
        wide = (columns + LANES - 1) // LANES * LANES
        lanes = 2 * bands * STRIDE
        rows = cells * width
        hbm = pl.BlockSpec(memory_space=pltpu.HBM)
        bf16, f32 = jnp.bfloat16, jnp.float32
        dma = pltpu.SemaphoreType.DMA
        operands = (coefficients, class_weight, diff_class, frag_cells, block_pattern)
        return pl.pallas_call(
            functools.partial(kernel, nk, bands, width, occupied, functions, blocks, cells),
            out_shape=jax.ShapeDtypeStruct((cells, 2, width, columns), f32),
            in_specs=[hbm] * 5,
            out_specs=pl.BlockSpec(memory_space=pltpu.VMEM),
            scratch_shapes=[
                pltpu.VMEM(coefficients.shape, bf16),
                *[pltpu.SMEM(x.shape, x.dtype) for x in operands[1:]],
                pltpu.VMEM((padded, 2 * lanes), bf16),
                pltpu.VMEM((n, 2 * width, padded), bf16),
                pltpu.VMEM((bands - 1, n, 2 * width, window), bf16),
                pltpu.VMEM((n, lanes, window), bf16),
                pltpu.VMEM((2 * cells, n, 2 * lanes), f32),
                pltpu.VMEM((rows, 2 * lanes), f32),
                pltpu.VMEM((rows, 2 * lanes), f32),
                pltpu.VMEM((n, rows, lanes), f32),
                pltpu.VMEM((2 * rows, wide), f32),
                pltpu.VMEM((2 * rows, wide), f32),
                dma((5,)),
                dma((n // 2, 2)), dma((n // 2, 2)), dma((n // 2, 2)), dma((n // 2, 2)),
                dma((bands - 1, n)), dma((bands - 1, n)),
                dma((n - 1,)), dma((n - 1,)), dma((3,)), dma((3,)),
            ],
            compiler_params=pltpu.CompilerParams(
                collective_id=0, has_side_effects=True, vmem_limit_bytes=63 * 2**20),
            cost_estimate=pl.CostEstimate(
                flops=8 * n * width * lanes * padded, bytes_accessed=8 * n * width * padded, transcendentals=0),
            name="exchange",
        )(*operands)

    placed = (P("ka", None, None, None), P(), P(), P(), P())
    return jax.shard_map(
        shards, mesh=mesh, in_specs=placed, out_specs=P(None, None, "band", "ka"), check_vma=False)
```

```python
import functools
import math

import jax
import jax.numpy as jnp
from jax import lax
from jax.experimental import pallas as pl
from jax.experimental.pallas import tpu as pltpu
from jax.sharding import PartitionSpec as P

MESH = pl.DeviceIdType.MESH
LANES = 128
STRIDE = 32


def kernel(nk, bands, width, occupied, functions, blocks, cells,
           own_hbm, weight_hbm, classes_hbm, frag_hbm, pattern_hbm, out,
           own, weight, classes, frag, pattern,
           sel, slots, near, stack, turn, acc, acc_in, packed, part, part_in,
           in_s, right_s, right_r, left_s, left_r, win_s, win_r, gat_s, gat_r, one_s, one_r):
    n = nk // 2
    half = n // 2
    ka, band = lax.axis_index("ka"), lax.axis_index("band")
    chip, core = ka // 2, ka % 2
    padded = slots.shape[2]
    tiles = padded // LANES
    first = (tiles + 1) // 2 * LANES
    chunks = (pl.ds(0, first), pl.ds(first, padded - first))
    window, wide = near.shape[3], stack.shape[3]
    columns = functions // nk
    lanes = 2 * bands * STRIDE
    rows = cells * width
    f32, bf16 = jnp.float32, jnp.bfloat16

    operands = (own_hbm, weight_hbm, classes_hbm, frag_hbm, pattern_hbm)
    fetches = [pltpu.make_async_copy(src, dst, in_s.at[i])
               for i, (src, dst) in enumerate(zip(operands, (own, weight, classes, frag, pattern)))]
    for fetch in fetches:
        fetch.start()

    def chip_at(ring):
        return jnp.where(ring < half, 2 * ring, 2 * (n - 1 - ring) + 1)

    row, odd = chip // 2, chip % 2
    ring = jnp.where(odd == 0, row, n - 1 - row)

    def wrap(x):
        x = jnp.where(x >= n, x - n, x)
        return jnp.where(x < 0, x + n, x)

    members = [2 * chip_at(wrap(ring + offset)) + core for offset in range(n)]

    def member(offset):
        return members[offset % n]

    sibling = 2 * chip + 1 - core
    barrier = pltpu.get_barrier_semaphore()
    for offset in range(1, n):
        pl.semaphore_signal(barrier, inc=1, device_id=(member(offset), band), device_id_type=MESH)
    pl.semaphore_signal(barrier, inc=1, device_id=(sibling, band), device_id_type=MESH)
    for offset in range(1, bands):
        pl.semaphore_signal(barrier, inc=1, device_id=(ka, (band + offset) % bands), device_id_type=MESH)

    def dot(a, b):
        return jnp.dot(a, b, preferred_element_type=f32)

    def iotas(shape):
        return (lax.broadcasted_iota(jnp.int32, shape, 0), lax.broadcasted_iota(jnp.int32, shape, 1))

    slots[0, :, padded - LANES:] = jnp.zeros((2 * width, LANES), bf16)
    r, c = iotas((2 * width, occupied))
    c = c - band * width
    pick_re = jnp.where((c >= 0) & (c < width) & (c == r), 1.0, 0.0).astype(bf16)
    pick_im = jnp.where((c >= 0) & (c < width) & (c == r - width), 1.0, 0.0).astype(bf16)
    fetches[0].wait()
    re, im = own[0, 0], own[0, 1]
    slots[0, :, :functions] = (dot(pick_re, re) + dot(pick_im, im)).astype(bf16)

    pl.semaphore_wait(barrier, n - 1 + 1 + bands - 1)

    def ring_copy(to_right, s, h):
        if to_right:
            src, dst, ss, rs, to = jnp.maximum(2 * s - 3, 0), 2 * s - 1, right_s, right_r, member(1)
        else:
            dst = jnp.where(s == half, n - 1, 2 * s)
            src, ss, rs, to = 2 * s - 2, left_s, left_r, member(-1)
        return pltpu.make_async_remote_copy(
            src_ref=slots.at[src, :, chunks[h]], dst_ref=slots.at[dst, :, chunks[h]],
            send_sem=ss.at[s - 1, h], recv_sem=rs.at[s - 1, h],
            device_id=(to, band), device_id_type=MESH)

    def steps(to_right, h):
        return half if h == (0 if to_right else 1) else half - 1

    start = pl.multiple_of(jnp.minimum(chip * 2 * columns // LANES, tiles - window // LANES) * LANES, LANES)

    def window_copy(g, t):
        return pltpu.make_async_remote_copy(
            src_ref=slots.at[t, :, pl.ds(start, window)], dst_ref=near.at[g - 1, t],
            send_sem=win_s.at[g - 1, t], recv_sem=win_r.at[g - 1, t],
            device_id=(ka, (band + g) % bands), device_id_type=MESH)

    def spread(t):
        for g in range(1, bands):
            window_copy(g, t).start()

    for h in range(2):
        for side in (True, False):
            ring_copy(side, 1, h).start()
    spread(0)

    r, c = iotas((occupied, lanes))
    hits = [jnp.zeros(r.shape, f32), jnp.zeros(r.shape, f32)]
    for ri in range(2):
        for g in range(bands):
            low = (ri * bands + g) * STRIDE
            inside = (c >= low) & (c < low + width)
            hits[ri] = jnp.where(inside & (r - ((band - g + bands) % bands) * width == c - low), 1.0, hits[ri])
    mine = pl.ds(pl.multiple_of(core * lanes, LANES), lanes)
    sel[padded - LANES:, mine] = jnp.zeros((LANES, lanes), bf16)

    def turned(value, hit):
        return lax.dot_general(value, hit.astype(bf16), (((0,), (0,)), ((), ())), preferred_element_type=f32)

    sel[:functions, mine] = (turned(re, hits[0]) + turned(im, hits[1])).astype(bf16)
    sel_copy = pltpu.make_async_remote_copy(
        src_ref=sel.at[:, mine], dst_ref=sel.at[:, mine], send_sem=one_s.at[0], recv_sem=one_r.at[0],
        device_id=(sibling, band), device_id_type=MESH)
    sel_copy.start()
    for fetch in fetches[1:]:
        fetch.wait()

    at = lax.broadcasted_iota(jnp.int32, (n, 2 * lanes), 0)
    where = wrap(jnp.where(at % 2 == 0, ring + at // 2, ring - at // 2 - 1))
    kpoint = (2 * chip_at(where) + core).astype(f32)
    lane = lax.broadcasted_iota(jnp.int32, (n, 2 * lanes), 1)
    sign = jnp.where(lane % lanes < lanes // 2, 1.0, -1.0)
    for f in range(cells):
        turns = kpoint * (frag[f].astype(f32) / nk)
        angle = 2.0 * math.pi * (turns - jnp.floor(turns))
        turn[f] = jnp.cos(angle) / nk
        turn[cells + f] = sign * jnp.sin(angle) / nk
    column = lax.broadcasted_iota(jnp.int32, (width, wide), 1) + ka * columns
    block = functions // blocks
    masks = []
    for f in range(cells):
        mask = jnp.zeros((width, wide), f32)
        for i in range(blocks):
            keep = (column >= i * block) & (column < (i + 1) * block)
            mask = jnp.where(keep, pattern[f, i].astype(f32), mask)
        masks.append(mask)

    def swap(x):
        return pltpu.roll(x, lanes // 2, 1)

    def swap_both(x):
        return jnp.concatenate([swap(x[:, :lanes]), swap(x[:, lanes:])], 1)

    own_lane = lax.broadcasted_iota(jnp.int32, (width, 2 * lanes), 1)
    signs = jnp.where(own_lane % lanes < lanes // 2, 1.0, -1.0)

    def product_of(i, h):
        return dot(slots[pl.ds(2 * i, 2), :, chunks[h]].reshape(4 * width, -1), sel[chunks[h], :])

    def overlap(i, product):
        for side in range(2):
            low = 2 * width * side
            k = 2 * chip_at(wrap(ring - i - 1 if side else ring + i)) + core
            value = product[low:low + width] + signs * swap_both(product[low + width:low + 2 * width])
            scale = jnp.where(own_lane < lanes, weight[classes[k, 2 * chip]], weight[classes[k, 2 * chip + 1]])
            value = (scale / functions * value).astype(bf16).astype(f32)
            other = swap_both(value)
            at = pl.ds(2 * i + side, 1)
            acc[...] += jnp.concatenate(
                [turn[f, at, :] * value + turn[cells + f, at, :] * other for f in range(cells)], 0)

    r, c = iotas((lanes, 2 * width))
    placers = []
    for g in range(bands):
        a, b = g * STRIDE, (bands + g) * STRIDE
        hit = ((c < width) & (r == a + c)) | ((c >= width) & (r == b + c - width))
        placers.append(jnp.where(hit, 1.0, 0.0).astype(bf16))

    offset = chip * 2 * columns - start

    def place(t):
        value = dot(placers[0], slots[t, :, pl.ds(start, window)])
        for g in range(1, bands):
            window_copy(g, t).wait_recv()
            value = value + dot(placers[g], near[g - 1, t])
        for c in range(2):
            stack[c, t] = pltpu.roll(value, window - offset - (core if c else 1 - core) * columns, 1)[:, :wide].astype(bf16)

    acc[...] = jnp.zeros((rows, 2 * lanes), f32)
    sel_copy.wait()

    @pl.loop(0, half)
    def _(i):
        s = i + 1
        for h in range(2):
            for side in (True, False):
                last = steps(side, h)

                @pl.when(s <= last)
                def _():
                    ring_copy(side, s, h).wait_recv()

                @pl.when(s < last)
                def _():
                    ring_copy(side, s + 1, h).start()
            if h == 0:
                product = product_of(i, 0)
        spread(2 * s - 1)

        @pl.when(s < half)
        def _():
            spread(2 * s)

        overlap(i, product + product_of(i, 1))

    theirs = pl.ds(pl.multiple_of((1 - core) * lanes, LANES), lanes)
    acc_copy = pltpu.make_async_remote_copy(
        src_ref=acc.at[:, theirs], dst_ref=acc_in, send_sem=one_s.at[1], recv_sem=one_r.at[1],
        device_id=(sibling, band), device_id_type=MESH)
    acc_copy.start()
    acc_copy.wait_recv()
    packed[0] = acc[:, mine] + acc_in[...]

    def place_at(receiver, source):
        t = wrap(receiver - source)
        return jnp.where((t > 0) & (t <= half), 2 * t - 1, jnp.where(t == 0, 0, 2 * (n - t)))

    def ring_of(line, side):
        return jnp.where(side == 0, line, n - 1 - line)

    def line_at(d):
        line = jnp.where(row + d >= half, row + d - half, row + d)
        return jnp.where(line < 0, line + half, line)

    def gather_copy(d):
        line = line_at(d)
        return pltpu.make_async_remote_copy(
            src_ref=packed.at[0], dst_ref=packed.at[place_at(ring_of(line, odd), ring)],
            send_sem=gat_s.at[d - 1], recv_sem=gat_r.at[d - 1],
            device_id=(2 * (2 * line + odd) + core, band), device_id_type=MESH)

    def across_copy(d):
        source = ring_of(line_at(-d), odd)
        return pltpu.make_async_remote_copy(
            src_ref=packed.at[place_at(ring, source)], dst_ref=packed.at[place_at(n - 1 - ring, source)],
            send_sem=gat_s.at[half - 1 + d], recv_sem=gat_r.at[half - 1 + d],
            device_id=(2 * (chip + 1 - 2 * odd) + core, band), device_id_type=MESH)

    across_copy(0).start()
    for d in range(1, half):
        gather_copy(d).start()
    pl.loop(0, n // 2)(place)
    for d in range(1, half):
        gather_copy(d).wait_recv()
        across_copy(d).start()
    pl.loop(n // 2, n)(place)

    @pl.loop(1, half + 1)
    def _(s):
        for h in range(2):
            for side in (True, False):
                @pl.when(s <= steps(side, h))
                def _():
                    ring_copy(side, s, h).wait_send()

    @pl.loop(0, n)
    def _(t):
        for g in range(1, bands):
            window_copy(g, t).wait_send()

    acc_copy.wait_send()
    for d in range(half):
        across_copy(d).wait_recv()

    rotated = lax.broadcasted_iota(jnp.int32, (rows, lanes), 1)
    flip = jnp.where(rotated < lanes // 2, -1.0, 1.0)
    real = [packed[t] for t in range(n)]
    left = jnp.concatenate(
        [jnp.concatenate(real, 1), jnp.concatenate([flip * swap(x) for x in real], 1)], 0)
    high = left.astype(bf16)
    low = (left - high.astype(f32)).astype(bf16)
    factors = jnp.concatenate([high, low], 0)

    def part_of(c):
        value = dot(factors, stack[c].reshape(n * lanes, wide))
        return value[:2 * rows] + value[2 * rows:]

    part[...] = part_of(0)
    part_copy = pltpu.make_async_remote_copy(
        src_ref=part, dst_ref=part_in, send_sem=one_s.at[2], recv_sem=one_r.at[2],
        device_id=(sibling, band), device_id_type=MESH)
    part_copy.start()
    kept = part_of(1)
    part_copy.wait_recv()
    whole = kept + part_in[...]
    for ri in range(2):
        for f in range(cells):
            spot = (ri * cells + f) * width
            out[f, :, ri, :] = (whole[spot:spot + width] * masks[f])[:, :columns]

    for d in range(1, half):
        gather_copy(d).wait_send()
    for d in range(half):
        across_copy(d).wait_send()
    part_copy.wait_send()


def solution(mesh):
    nk, bands = mesh.shape["ka"], mesh.shape["band"]
    n = nk // 2

    def shards(coefficients, class_weight, diff_class, frag_cells, block_pattern):
        occupied, functions = coefficients.shape[2:]
        width = occupied // bands
        cells, blocks = block_pattern.shape
        padded = (functions + LANES - 1) // LANES * LANES
        columns = functions // nk
        window = (2 * columns + 2 * LANES - 2) // LANES * LANES
        wide = (columns + LANES - 1) // LANES * LANES
        lanes = 2 * bands * STRIDE
        rows = cells * width
        hbm = pl.BlockSpec(memory_space=pltpu.HBM)
        bf16, f32 = jnp.bfloat16, jnp.float32
        dma = pltpu.SemaphoreType.DMA
        operands = (coefficients, class_weight, diff_class, frag_cells, block_pattern)
        result = pl.pallas_call(
            functools.partial(kernel, nk, bands, width, occupied, functions, blocks, cells),
            out_shape=jax.ShapeDtypeStruct((cells, width, 2, columns), f32),
            in_specs=[hbm] * 5,
            out_specs=pl.BlockSpec(memory_space=pltpu.VMEM),
            scratch_shapes=[
                pltpu.VMEM(coefficients.shape, bf16),
                *[pltpu.SMEM(x.shape, x.dtype) for x in operands[1:]],
                pltpu.VMEM((padded, 2 * lanes), bf16),
                pltpu.VMEM((n, 2 * width, padded), bf16),
                pltpu.VMEM((bands - 1, n, 2 * width, window), bf16),
                pltpu.VMEM((2, n, lanes, wide), bf16),
                pltpu.VMEM((2 * cells, n, 2 * lanes), f32),
                pltpu.VMEM((rows, 2 * lanes), f32),
                pltpu.VMEM((rows, lanes), f32),
                pltpu.VMEM((n, rows, lanes), f32),
                pltpu.VMEM((2 * rows, wide), f32),
                pltpu.VMEM((2 * rows, wide), f32),
                dma((5,)),
                dma((n // 2, 2)), dma((n // 2, 2)), dma((n // 2, 2)), dma((n // 2, 2)),
                dma((bands - 1, n)), dma((bands - 1, n)),
                dma((n - 1,)), dma((n - 1,)), dma((3,)), dma((3,)),
            ],
            compiler_params=pltpu.CompilerParams(
                collective_id=0, has_side_effects=True, vmem_limit_bytes=63 * 2**20),
            cost_estimate=pl.CostEstimate(
                flops=8 * n * width * lanes * padded, bytes_accessed=8 * n * width * padded, transcendentals=0),
            name="exchange",
        )(*operands)
        return jnp.swapaxes(result, 1, 2)

    placed = (P("ka", None, None, None), P(), P(), P(), P())
    return jax.shard_map(
        shards, mesh=mesh, in_specs=placed, out_specs=P(None, None, "band", "ka"), check_vma=False)
```

```python
import functools
import math

import jax
import jax.numpy as jnp
from jax import lax
from jax.experimental import pallas as pl
from jax.experimental.pallas import tpu as pltpu
from jax.sharding import PartitionSpec as P

MESH = pl.DeviceIdType.MESH
LANES = 128
STRIDE = 32


def kernel(nk, bands, width, occupied, functions, blocks, cells,
           own_hbm, weight_hbm, classes_hbm, frag_hbm, pattern_hbm, out,
           own, weight, classes, frag, pattern,
           sel, slots, near, stack, turn, acc, acc_in, packed, part, part_in,
           in_s, right_s, right_r, left_s, left_r, win_s, win_r, gat_s, gat_r, one_s, one_r):
    n = nk // 2
    half = n // 2
    ka, band = lax.axis_index("ka"), lax.axis_index("band")
    chip, core = ka // 2, ka % 2
    padded = slots.shape[2]
    tiles = padded // LANES
    first = (tiles + 1) // 2 * LANES
    chunks = (pl.ds(0, first), pl.ds(first, padded - first))
    window, wide = near.shape[3], stack.shape[3]
    columns = functions // nk
    lanes = 2 * bands * STRIDE
    rows = cells * width
    f32, bf16 = jnp.float32, jnp.bfloat16

    operands = (own_hbm, weight_hbm, classes_hbm, frag_hbm, pattern_hbm)
    fetches = [pltpu.make_async_copy(src, dst, in_s.at[i])
               for i, (src, dst) in enumerate(zip(operands, (own, weight, classes, frag, pattern)))]
    for fetch in fetches:
        fetch.start()

    def chip_at(ring):
        return jnp.where(ring < half, 2 * ring, 2 * (n - 1 - ring) + 1)

    row, odd = chip // 2, chip % 2
    ring = jnp.where(odd == 0, row, n - 1 - row)

    def wrap(x):
        x = jnp.where(x >= n, x - n, x)
        return jnp.where(x < 0, x + n, x)

    members = [2 * chip_at(wrap(ring + offset)) + core for offset in range(n)]

    def member(offset):
        return members[offset % n]

    sibling = 2 * chip + 1 - core
    barrier = pltpu.get_barrier_semaphore()
    for offset in range(1, n):
        pl.semaphore_signal(barrier, inc=1, device_id=(member(offset), band), device_id_type=MESH)
    pl.semaphore_signal(barrier, inc=1, device_id=(sibling, band), device_id_type=MESH)
    for offset in range(1, bands):
        pl.semaphore_signal(barrier, inc=1, device_id=(ka, (band + offset) % bands), device_id_type=MESH)

    def dot(a, b):
        return jnp.dot(a, b, preferred_element_type=f32)

    def iotas(shape):
        return (lax.broadcasted_iota(jnp.int32, shape, 0), lax.broadcasted_iota(jnp.int32, shape, 1))

    slots[0, :, padded - LANES:] = jnp.zeros((2 * width, LANES), bf16)
    r, c = iotas((2 * width, occupied))
    c = c - band * width
    pick_re = jnp.where((c >= 0) & (c < width) & (c == r), 1.0, 0.0).astype(bf16)
    pick_im = jnp.where((c >= 0) & (c < width) & (c == r - width), 1.0, 0.0).astype(bf16)
    fetches[0].wait()
    re, im = own[0, 0], own[0, 1]
    slots[0, :, :functions] = (dot(pick_re, re) + dot(pick_im, im)).astype(bf16)

    pl.semaphore_wait(barrier, n - 1 + 1 + bands - 1)

    def ring_copy(to_right, s, h):
        if to_right:
            src, dst, ss, rs, to = jnp.maximum(2 * s - 3, 0), 2 * s - 1, right_s, right_r, member(1)
        else:
            dst = jnp.where(s == half, n - 1, 2 * s)
            src, ss, rs, to = 2 * s - 2, left_s, left_r, member(-1)
        return pltpu.make_async_remote_copy(
            src_ref=slots.at[src, :, chunks[h]], dst_ref=slots.at[dst, :, chunks[h]],
            send_sem=ss.at[s - 1, h], recv_sem=rs.at[s - 1, h],
            device_id=(to, band), device_id_type=MESH)

    def steps(to_right, h):
        return half if h == (0 if to_right else 1) else half - 1

    start = pl.multiple_of(jnp.minimum(chip * 2 * columns // LANES, tiles - window // LANES) * LANES, LANES)

    def window_copy(g, t):
        return pltpu.make_async_remote_copy(
            src_ref=slots.at[t, :, pl.ds(start, window)], dst_ref=near.at[g - 1, t],
            send_sem=win_s.at[g - 1, t], recv_sem=win_r.at[g - 1, t],
            device_id=(ka, (band + g) % bands), device_id_type=MESH)

    def spread(t):
        for g in range(1, bands):
            window_copy(g, t).start()

    for h in range(2):
        for side in (True, False):
            ring_copy(side, 1, h).start()
    spread(0)

    r, c = iotas((occupied, lanes))
    hits = [jnp.zeros(r.shape, f32), jnp.zeros(r.shape, f32)]
    for ri in range(2):
        for g in range(bands):
            low = (ri * bands + g) * STRIDE
            inside = (c >= low) & (c < low + width)
            hits[ri] = jnp.where(inside & (r - ((band - g + bands) % bands) * width == c - low), 1.0, hits[ri])
    mine = pl.ds(pl.multiple_of(core * lanes, LANES), lanes)
    sel[padded - LANES:, mine] = jnp.zeros((LANES, lanes), bf16)

    def turned(value, hit):
        return lax.dot_general(value, hit.astype(bf16), (((0,), (0,)), ((), ())), preferred_element_type=f32)

    sel[:functions, mine] = (turned(re, hits[0]) + turned(im, hits[1])).astype(bf16)
    sel_copy = pltpu.make_async_remote_copy(
        src_ref=sel.at[:, mine], dst_ref=sel.at[:, mine], send_sem=one_s.at[0], recv_sem=one_r.at[0],
        device_id=(sibling, band), device_id_type=MESH)
    sel_copy.start()
    for fetch in fetches[1:]:
        fetch.wait()

    at = lax.broadcasted_iota(jnp.int32, (n, 2 * lanes), 0)
    where = wrap(jnp.where(at % 2 == 0, ring + at // 2, ring - at // 2 - 1))
    kpoint = (2 * chip_at(where) + core).astype(f32)
    lane = lax.broadcasted_iota(jnp.int32, (n, 2 * lanes), 1)
    sign = jnp.where(lane % lanes < lanes // 2, 1.0, -1.0)
    for f in range(cells):
        turns = kpoint * (frag[f].astype(f32) / nk)
        angle = 2.0 * math.pi * (turns - jnp.floor(turns))
        turn[f] = jnp.cos(angle) / nk
        turn[cells + f] = sign * jnp.sin(angle) / nk
    column = lax.broadcasted_iota(jnp.int32, (width, wide), 1) + ka * columns
    block = functions // blocks
    masks = []
    for f in range(cells):
        mask = jnp.zeros((width, wide), f32)
        for i in range(blocks):
            keep = (column >= i * block) & (column < (i + 1) * block)
            mask = jnp.where(keep, pattern[f, i].astype(f32), mask)
        masks.append(mask)

    def swap(x):
        return pltpu.roll(x, lanes // 2, 1)

    def swap_both(x):
        return jnp.concatenate([swap(x[:, :lanes]), swap(x[:, lanes:])], 1)

    own_lane = lax.broadcasted_iota(jnp.int32, (width, 2 * lanes), 1)
    signs = jnp.where(own_lane % lanes < lanes // 2, 1.0, -1.0)

    def product_of(i, h):
        return dot(slots[pl.ds(2 * i, 2), :, chunks[h]].reshape(4 * width, -1), sel[chunks[h], :])

    def overlap(i, product):
        for side in range(2):
            low = 2 * width * side
            k = 2 * chip_at(wrap(ring - i - 1 if side else ring + i)) + core
            value = product[low:low + width] + signs * swap_both(product[low + width:low + 2 * width])
            scale = jnp.where(own_lane < lanes, weight[classes[k, 2 * chip]], weight[classes[k, 2 * chip + 1]])
            value = (scale / functions * value).astype(bf16).astype(f32)
            other = swap_both(value)
            at = pl.ds(2 * i + side, 1)
            acc[...] += jnp.concatenate(
                [turn[f, at, :] * value + turn[cells + f, at, :] * other for f in range(cells)], 0)

    r, c = iotas((lanes, 2 * width))
    placers = []
    for g in range(bands):
        a, b = g * STRIDE, (bands + g) * STRIDE
        hit = ((c < width) & (r == a + c)) | ((c >= width) & (r == b + c - width))
        placers.append(jnp.where(hit, 1.0, 0.0).astype(bf16))

    offset = chip * 2 * columns - start

    def place(t):
        value = dot(placers[0], slots[t, :, pl.ds(start, window)])
        for g in range(1, bands):
            window_copy(g, t).wait_recv()
            value = value + dot(placers[g], near[g - 1, t])
        for c in range(2):
            stack[c, t] = pltpu.roll(value, window - offset - (core if c else 1 - core) * columns, 1)[:, :wide].astype(bf16)

    acc[...] = jnp.zeros((rows, 2 * lanes), f32)
    sel_copy.wait()

    @pl.loop(0, half)
    def _(i):
        s = i + 1
        for h in range(2):
            for side in (True, False):
                last = steps(side, h)

                @pl.when(s <= last)
                def _():
                    ring_copy(side, s, h).wait_recv()

                @pl.when(s < last)
                def _():
                    ring_copy(side, s + 1, h).start()
            if h == 0:
                product = product_of(i, 0)
        spread(2 * s - 1)

        @pl.when(s < half)
        def _():
            spread(2 * s)

        overlap(i, product + product_of(i, 1))

        @pl.when(i > 0)
        def _():
            place(2 * i - 2)
            place(2 * i - 1)

    theirs = pl.ds(pl.multiple_of((1 - core) * lanes, LANES), lanes)
    acc_copy = pltpu.make_async_remote_copy(
        src_ref=acc.at[:, theirs], dst_ref=acc_in, send_sem=one_s.at[1], recv_sem=one_r.at[1],
        device_id=(sibling, band), device_id_type=MESH)
    acc_copy.start()
    acc_copy.wait_recv()
    packed[0] = acc[:, mine] + acc_in[...]

    def place_of(t):
        return 2 * t - 1 if 0 < t <= half else 2 * ((n - t) % n)

    def gather_copy(t):
        return pltpu.make_async_remote_copy(
            src_ref=packed.at[0], dst_ref=packed.at[place_of(t)], send_sem=gat_s.at[t - 1], recv_sem=gat_r.at[t - 1],
            device_id=(member(t), band), device_id_type=MESH)

    order = sorted(range(1, n), key=lambda t: -min(t, n - t))
    for t in order:
        gather_copy(t).start()
    place(n - 2)
    place(n - 1)

    @pl.loop(1, half + 1)
    def _(s):
        for h in range(2):
            for side in (True, False):
                @pl.when(s <= steps(side, h))
                def _():
                    ring_copy(side, s, h).wait_send()

    @pl.loop(0, n)
    def _(t):
        for g in range(1, bands):
            window_copy(g, t).wait_send()

    acc_copy.wait_send()
    for t in order:
        gather_copy(t).wait_recv()

    rotated = lax.broadcasted_iota(jnp.int32, (rows, lanes), 1)
    flip = jnp.where(rotated < lanes // 2, -1.0, 1.0)
    real = [packed[t] for t in range(n)]
    left = jnp.concatenate(
        [jnp.concatenate(real, 1), jnp.concatenate([flip * swap(x) for x in real], 1)], 0)
    high = left.astype(bf16)
    low = (left - high.astype(f32)).astype(bf16)
    factors = jnp.concatenate([high, low], 0)

    def part_of(c):
        value = dot(factors, stack[c].reshape(n * lanes, wide))
        return value[:2 * rows] + value[2 * rows:]

    part[...] = part_of(0)
    part_copy = pltpu.make_async_remote_copy(
        src_ref=part, dst_ref=part_in, send_sem=one_s.at[2], recv_sem=one_r.at[2],
        device_id=(sibling, band), device_id_type=MESH)
    part_copy.start()
    kept = part_of(1)
    part_copy.wait_recv()
    whole = kept + part_in[...]
    for ri in range(2):
        for f in range(cells):
            spot = (ri * cells + f) * width
            out[f, ri] = (whole[spot:spot + width] * masks[f])[:, :columns]

    for t in order:
        gather_copy(t).wait_send()
    part_copy.wait_send()


def solution(mesh):
    nk, bands = mesh.shape["ka"], mesh.shape["band"]
    n = nk // 2

    def shards(coefficients, class_weight, diff_class, frag_cells, block_pattern):
        occupied, functions = coefficients.shape[2:]
        width = occupied // bands
        cells, blocks = block_pattern.shape
        padded = (functions + LANES - 1) // LANES * LANES
        columns = functions // nk
        window = (2 * columns + 2 * LANES - 2) // LANES * LANES
        wide = (columns + LANES - 1) // LANES * LANES
        lanes = 2 * bands * STRIDE
        rows = cells * width
        hbm = pl.BlockSpec(memory_space=pltpu.HBM)
        bf16, f32 = jnp.bfloat16, jnp.float32
        dma = pltpu.SemaphoreType.DMA
        operands = (coefficients, class_weight, diff_class, frag_cells, block_pattern)
        return pl.pallas_call(
            functools.partial(kernel, nk, bands, width, occupied, functions, blocks, cells),
            out_shape=jax.ShapeDtypeStruct((cells, 2, width, columns), f32),
            in_specs=[hbm] * 5,
            out_specs=pl.BlockSpec(memory_space=pltpu.VMEM),
            scratch_shapes=[
                pltpu.VMEM(coefficients.shape, bf16),
                *[pltpu.SMEM(x.shape, x.dtype) for x in operands[1:]],
                pltpu.VMEM((padded, 2 * lanes), bf16),
                pltpu.VMEM((n, 2 * width, padded), bf16),
                pltpu.VMEM((bands - 1, n, 2 * width, window), bf16),
                pltpu.VMEM((2, n, lanes, wide), bf16),
                pltpu.VMEM((2 * cells, n, 2 * lanes), f32),
                pltpu.VMEM((rows, 2 * lanes), f32),
                pltpu.VMEM((rows, lanes), f32),
                pltpu.VMEM((n, rows, lanes), f32),
                pltpu.VMEM((2 * rows, wide), f32),
                pltpu.VMEM((2 * rows, wide), f32),
                dma((5,)),
                dma((n // 2, 2)), dma((n // 2, 2)), dma((n // 2, 2)), dma((n // 2, 2)),
                dma((bands - 1, n)), dma((bands - 1, n)),
                dma((n - 1,)), dma((n - 1,)), dma((3,)), dma((3,)),
            ],
            compiler_params=pltpu.CompilerParams(
                collective_id=0, has_side_effects=True, vmem_limit_bytes=63 * 2**20),
            cost_estimate=pl.CostEstimate(
                flops=8 * n * width * lanes * padded, bytes_accessed=8 * n * width * padded, transcendentals=0),
            name="exchange",
        )(*operands)

    placed = (P("ka", None, None, None), P(), P(), P(), P())
    return jax.shard_map(
        shards, mesh=mesh, in_specs=placed, out_specs=P(None, None, "band", "ka"), check_vma=False)
```

```python
import functools
import math

import jax
import jax.numpy as jnp
from jax import lax
from jax.experimental import pallas as pl
from jax.experimental.pallas import tpu as pltpu
from jax.sharding import PartitionSpec as P

MESH = pl.DeviceIdType.MESH
LANES = 128
STRIDE = 32


def kernel(nk, bands, width, occupied, functions, blocks, cells,
           own_hbm, weight_hbm, classes_hbm, frag_hbm, pattern_hbm, out,
           own, weight, classes, frag, pattern,
           sel, slots, near, stack, turn, acc, acc_in, packed, part, part_in,
           in_s, right_s, right_r, left_s, left_r, win_s, win_r, gat_s, gat_r, one_s, one_r):
    n = nk // 2
    half = n // 2
    ka, band = lax.axis_index("ka"), lax.axis_index("band")
    chip, core = ka // 2, ka % 2
    padded = slots.shape[2]
    tiles = padded // LANES
    first = (tiles + 1) // 2 * LANES
    chunks = (pl.ds(0, first), pl.ds(first, padded - first))
    window, wide = near.shape[3], stack.shape[3]
    columns = functions // nk
    lanes = 2 * bands * STRIDE
    rows = cells * width
    f32, bf16 = jnp.float32, jnp.bfloat16

    operands = (own_hbm, weight_hbm, classes_hbm, frag_hbm, pattern_hbm)
    fetches = [pltpu.make_async_copy(src, dst, in_s.at[i])
               for i, (src, dst) in enumerate(zip(operands, (own, weight, classes, frag, pattern)))]
    for fetch in fetches:
        fetch.start()

    def chip_at(ring):
        return jnp.where(ring < half, 2 * ring, 2 * (n - 1 - ring) + 1)

    row, odd = chip // 2, chip % 2
    ring = jnp.where(odd == 0, row, n - 1 - row)

    def wrap(x):
        x = jnp.where(x >= n, x - n, x)
        return jnp.where(x < 0, x + n, x)

    members = [2 * chip_at(wrap(ring + offset)) + core for offset in range(n)]

    def member(offset):
        return members[offset % n]

    sibling = 2 * chip + 1 - core
    barrier = pltpu.get_barrier_semaphore()
    for offset in (1, -1):
        pl.semaphore_signal(barrier, inc=1, device_id=(member(offset), band), device_id_type=MESH)
    pl.semaphore_signal(barrier, inc=1, device_id=(sibling, band), device_id_type=MESH)
    for offset in range(1, bands):
        pl.semaphore_signal(barrier, inc=1, device_id=(ka, (band + offset) % bands), device_id_type=MESH)

    def dot(a, b):
        return jnp.dot(a, b, preferred_element_type=f32)

    def iotas(shape):
        return (lax.broadcasted_iota(jnp.int32, shape, 0), lax.broadcasted_iota(jnp.int32, shape, 1))

    slots[0, :, padded - LANES:] = jnp.zeros((2 * width, LANES), bf16)
    r, c = iotas((2 * width, occupied))
    c = c - band * width
    pick_re = jnp.where((c >= 0) & (c < width) & (c == r), 1.0, 0.0).astype(bf16)
    pick_im = jnp.where((c >= 0) & (c < width) & (c == r - width), 1.0, 0.0).astype(bf16)
    fetches[0].wait()
    re, im = own[0, 0], own[0, 1]
    slots[0, :, :functions] = (dot(pick_re, re) + dot(pick_im, im)).astype(bf16)

    pl.semaphore_wait(barrier, 2 + 1 + bands - 1)

    def ring_copy(to_right, s, h):
        if to_right:
            src, dst, ss, rs, to = jnp.maximum(2 * s - 3, 0), 2 * s - 1, right_s, right_r, member(1)
        else:
            dst = jnp.where(s == half, n - 1, 2 * s)
            src, ss, rs, to = 2 * s - 2, left_s, left_r, member(-1)
        return pltpu.make_async_remote_copy(
            src_ref=slots.at[src, :, chunks[h]], dst_ref=slots.at[dst, :, chunks[h]],
            send_sem=ss.at[s - 1, h], recv_sem=rs.at[s - 1, h],
            device_id=(to, band), device_id_type=MESH)

    def steps(to_right, h):
        return half if h == (0 if to_right else 1) else half - 1

    start = pl.multiple_of(jnp.minimum(chip * 2 * columns // LANES, tiles - window // LANES) * LANES, LANES)

    def window_copy(g, t):
        return pltpu.make_async_remote_copy(
            src_ref=slots.at[t, :, pl.ds(start, window)], dst_ref=near.at[g - 1, t],
            send_sem=win_s.at[g - 1, t], recv_sem=win_r.at[g - 1, t],
            device_id=(ka, (band + g) % bands), device_id_type=MESH)

    def spread(t):
        for g in range(1, bands):
            window_copy(g, t).start()

    for h in range(2):
        for side in (True, False):
            ring_copy(side, 1, h).start()
    spread(0)

    r, c = iotas((occupied, lanes))
    hits = [jnp.zeros(r.shape, f32), jnp.zeros(r.shape, f32)]
    for ri in range(2):
        for g in range(bands):
            low = (ri * bands + g) * STRIDE
            inside = (c >= low) & (c < low + width)
            hits[ri] = jnp.where(inside & (r - ((band - g + bands) % bands) * width == c - low), 1.0, hits[ri])
    mine = pl.ds(pl.multiple_of(core * lanes, LANES), lanes)
    sel[padded - LANES:, mine] = jnp.zeros((LANES, lanes), bf16)

    def turned(value, hit):
        return lax.dot_general(value, hit.astype(bf16), (((0,), (0,)), ((), ())), preferred_element_type=f32)

    sel[:functions, mine] = (turned(re, hits[0]) + turned(im, hits[1])).astype(bf16)
    sel_copy = pltpu.make_async_remote_copy(
        src_ref=sel.at[:, mine], dst_ref=sel.at[:, mine], send_sem=one_s.at[0], recv_sem=one_r.at[0],
        device_id=(sibling, band), device_id_type=MESH)
    sel_copy.start()
    for fetch in fetches[1:]:
        fetch.wait()

    at = lax.broadcasted_iota(jnp.int32, (n, 2 * lanes), 0)
    where = wrap(jnp.where(at % 2 == 0, ring + at // 2, ring - at // 2 - 1))
    kpoint = (2 * chip_at(where) + core).astype(f32)
    lane = lax.broadcasted_iota(jnp.int32, (n, 2 * lanes), 1)
    sign = jnp.where(lane % lanes < lanes // 2, 1.0, -1.0)
    for f in range(cells):
        turns = kpoint * (frag[f].astype(f32) / nk)
        angle = 2.0 * math.pi * (turns - jnp.floor(turns))
        turn[f] = jnp.cos(angle) / nk
        turn[cells + f] = sign * jnp.sin(angle) / nk
    def swap(x):
        return pltpu.roll(x, lanes // 2, 1)

    def swap_both(x):
        return jnp.concatenate([swap(x[:, :lanes]), swap(x[:, lanes:])], 1)

    own_lane = lax.broadcasted_iota(jnp.int32, (width, 2 * lanes), 1)
    signs = jnp.where(own_lane % lanes < lanes // 2, 1.0, -1.0)

    def product_of(i, h):
        return dot(slots[pl.ds(2 * i, 2), :, chunks[h]].reshape(4 * width, -1), sel[chunks[h], :])

    def overlap(i, product):
        for side in range(2):
            low = 2 * width * side
            k = 2 * chip_at(wrap(ring - i - 1 if side else ring + i)) + core
            value = product[low:low + width] + signs * swap_both(product[low + width:low + 2 * width])
            scale = jnp.where(own_lane < lanes, weight[classes[k, 2 * chip]], weight[classes[k, 2 * chip + 1]])
            value = (scale / functions * value).astype(bf16).astype(f32)
            other = swap_both(value)
            at = pl.ds(2 * i + side, 1)
            acc[...] += jnp.concatenate(
                [turn[f, at, :] * value + turn[cells + f, at, :] * other for f in range(cells)], 0)

    r, c = iotas((lanes, 2 * width))
    placers = []
    for g in range(bands):
        a, b = g * STRIDE, (bands + g) * STRIDE
        hit = ((c < width) & (r == a + c)) | ((c >= width) & (r == b + c - width))
        placers.append(jnp.where(hit, 1.0, 0.0).astype(bf16))

    offset = chip * 2 * columns - start

    def place(t):
        value = dot(placers[0], slots[t, :, pl.ds(start, window)])
        for g in range(1, bands):
            window_copy(g, t).wait_recv()
            value = value + dot(placers[g], near[g - 1, t])
        for c in range(2):
            stack[c, t] = pltpu.roll(value, window - offset - (core if c else 1 - core) * columns, 1)[:, :wide].astype(bf16)

    acc[...] = jnp.zeros((rows, 2 * lanes), f32)

    @pl.loop(0, half)
    def _(i):
        s = i + 1
        for h in range(2):
            for side in (True, False):
                last = steps(side, h)

                @pl.when(s <= last)
                def _():
                    ring_copy(side, s, h).wait_recv()

                @pl.when(s < last)
                def _():
                    ring_copy(side, s + 1, h).start()
            if h == 0:
                @pl.when(i == 0)
                def _():
                    sel_copy.wait()

                product = product_of(i, 0)
        spread(2 * s - 1)

        @pl.when(s < half)
        def _():
            spread(2 * s)

        overlap(i, product + product_of(i, 1))

        @pl.when(i > 0)
        def _():
            place(2 * i - 2)
            place(2 * i - 1)

    theirs = pl.ds(pl.multiple_of((1 - core) * lanes, LANES), lanes)
    acc_copy = pltpu.make_async_remote_copy(
        src_ref=acc.at[:, theirs], dst_ref=acc_in, send_sem=one_s.at[1], recv_sem=one_r.at[1],
        device_id=(sibling, band), device_id_type=MESH)
    acc_copy.start()
    acc_copy.wait_recv()
    packed[0] = acc[:, mine] + acc_in[...]

    def place_of(t):
        return 2 * t - 1 if 0 < t <= half else 2 * ((n - t) % n)

    def gather_copy(t):
        return pltpu.make_async_remote_copy(
            src_ref=packed.at[0], dst_ref=packed.at[place_of(t)], send_sem=gat_s.at[t - 1], recv_sem=gat_r.at[t - 1],
            device_id=(member(t), band), device_id_type=MESH)

    order = sorted(range(1, n), key=lambda t: -min(t, n - t))
    for t in order:
        gather_copy(t).start()
    place(n - 2)
    place(n - 1)

    column = lax.broadcasted_iota(jnp.int32, (width, wide), 1) + ka * columns
    block = functions // blocks
    masks = []
    for f in range(cells):
        mask = jnp.zeros((width, wide), f32)
        for i in range(blocks):
            keep = (column >= i * block) & (column < (i + 1) * block)
            mask = jnp.where(keep, pattern[f, i].astype(f32), mask)
        masks.append(mask)

    @pl.loop(1, half + 1)
    def _(s):
        for h in range(2):
            for side in (True, False):
                @pl.when(s <= steps(side, h))
                def _():
                    ring_copy(side, s, h).wait_send()

    @pl.loop(0, n)
    def _(t):
        for g in range(1, bands):
            window_copy(g, t).wait_send()

    acc_copy.wait_send()
    for t in order:
        gather_copy(t).wait_recv()

    rotated = lax.broadcasted_iota(jnp.int32, (rows, lanes), 1)
    flip = jnp.where(rotated < lanes // 2, -1.0, 1.0)
    real = [packed[t] for t in range(n)]
    left = jnp.concatenate(
        [jnp.concatenate(real, 1), jnp.concatenate([flip * swap(x) for x in real], 1)], 0)
    high = left.astype(bf16)
    low = (left - high.astype(f32)).astype(bf16)
    factors = jnp.concatenate([high, low], 0)

    def part_of(c):
        value = dot(factors, stack[c].reshape(n * lanes, wide))
        return value[:2 * rows] + value[2 * rows:]

    part[...] = part_of(0)
    part_copy = pltpu.make_async_remote_copy(
        src_ref=part, dst_ref=part_in, send_sem=one_s.at[2], recv_sem=one_r.at[2],
        device_id=(sibling, band), device_id_type=MESH)
    part_copy.start()
    kept = part_of(1)
    part_copy.wait_recv()
    whole = kept + part_in[...]
    for ri in range(2):
        for f in range(cells):
            spot = (ri * cells + f) * width
            out[f, ri] = (whole[spot:spot + width] * masks[f])[:, :columns]

    for t in order:
        gather_copy(t).wait_send()
    part_copy.wait_send()


def solution(mesh):
    nk, bands = mesh.shape["ka"], mesh.shape["band"]
    n = nk // 2

    def shards(coefficients, class_weight, diff_class, frag_cells, block_pattern):
        occupied, functions = coefficients.shape[2:]
        width = occupied // bands
        cells, blocks = block_pattern.shape
        padded = (functions + LANES - 1) // LANES * LANES
        columns = functions // nk
        window = (2 * columns + 2 * LANES - 2) // LANES * LANES
        wide = (columns + LANES - 1) // LANES * LANES
        lanes = 2 * bands * STRIDE
        rows = cells * width
        hbm = pl.BlockSpec(memory_space=pltpu.HBM)
        bf16, f32 = jnp.bfloat16, jnp.float32
        dma = pltpu.SemaphoreType.DMA
        operands = (coefficients, class_weight, diff_class, frag_cells, block_pattern)
        return pl.pallas_call(
            functools.partial(kernel, nk, bands, width, occupied, functions, blocks, cells),
            out_shape=jax.ShapeDtypeStruct((cells, 2, width, columns), f32),
            in_specs=[hbm] * 5,
            out_specs=pl.BlockSpec(memory_space=pltpu.VMEM),
            scratch_shapes=[
                pltpu.VMEM(coefficients.shape, bf16),
                *[pltpu.SMEM(x.shape, x.dtype) for x in operands[1:]],
                pltpu.VMEM((padded, 2 * lanes), bf16),
                pltpu.VMEM((n, 2 * width, padded), bf16),
                pltpu.VMEM((bands - 1, n, 2 * width, window), bf16),
                pltpu.VMEM((2, n, lanes, wide), bf16),
                pltpu.VMEM((2 * cells, n, 2 * lanes), f32),
                pltpu.VMEM((rows, 2 * lanes), f32),
                pltpu.VMEM((rows, lanes), f32),
                pltpu.VMEM((n, rows, lanes), f32),
                pltpu.VMEM((2 * rows, wide), f32),
                pltpu.VMEM((2 * rows, wide), f32),
                dma((5,)),
                dma((n // 2, 2)), dma((n // 2, 2)), dma((n // 2, 2)), dma((n // 2, 2)),
                dma((bands - 1, n)), dma((bands - 1, n)),
                dma((n - 1,)), dma((n - 1,)), dma((3,)), dma((3,)),
            ],
            compiler_params=pltpu.CompilerParams(
                collective_id=0, has_side_effects=True, vmem_limit_bytes=63 * 2**20),
            cost_estimate=pl.CostEstimate(
                flops=8 * n * width * lanes * padded, bytes_accessed=8 * n * width * padded, transcendentals=0),
            name="exchange",
        )(*operands)

    placed = (P("ka", None, None, None), P(), P(), P(), P())
    return jax.shard_map(
        shards, mesh=mesh, in_specs=placed, out_specs=P(None, None, "band", "ka"), check_vma=False)
```

```python
import functools
import math

import jax
import jax.numpy as jnp
from jax import lax
from jax.experimental import pallas as pl
from jax.experimental.pallas import tpu as pltpu
from jax.sharding import PartitionSpec as P

MESH = pl.DeviceIdType.MESH
LANES = 128
STRIDE = 32


def kernel(nk, bands, width, occupied, functions, blocks, cells,
           own_hbm, weight_hbm, classes_hbm, frag_hbm, pattern_hbm, out,
           own, weight, classes, frag, pattern,
           sel, slots, near, stack, turn, acc, acc_in, packed, part, part_in,
           in_s, right_s, right_r, left_s, left_r, win_s, win_r, gat_s, gat_r, one_s, one_r):
    n = nk // 2
    half = n // 2
    ka, band = lax.axis_index("ka"), lax.axis_index("band")
    chip, core = ka // 2, ka % 2
    padded = slots.shape[2]
    tiles = padded // LANES
    first = (tiles + 1) // 2 * LANES
    chunks = (pl.ds(0, first), pl.ds(first, padded - first))
    window, wide = near.shape[3], stack.shape[3]
    columns = functions // nk
    lanes = 2 * bands * STRIDE
    rows = cells * width
    f32, bf16 = jnp.float32, jnp.bfloat16

    operands = (own_hbm, weight_hbm, classes_hbm, frag_hbm, pattern_hbm)
    fetches = [pltpu.make_async_copy(src, dst, in_s.at[i])
               for i, (src, dst) in enumerate(zip(operands, (own, weight, classes, frag, pattern)))]
    for fetch in fetches:
        fetch.start()

    def chip_at(ring):
        return jnp.where(ring < half, 2 * ring, 2 * (n - 1 - ring) + 1)

    row, odd = chip // 2, chip % 2
    ring = jnp.where(odd == 0, row, n - 1 - row)

    def wrap(x):
        x = jnp.where(x >= n, x - n, x)
        return jnp.where(x < 0, x + n, x)

    members = [2 * chip_at(wrap(ring + offset)) + core for offset in range(n)]

    def member(offset):
        return members[offset % n]

    sibling = 2 * chip + 1 - core
    barrier = pltpu.get_barrier_semaphore()
    for offset in (1, -1):
        pl.semaphore_signal(barrier, inc=1, device_id=(member(offset), band), device_id_type=MESH)
    pl.semaphore_signal(barrier, inc=1, device_id=(sibling, band), device_id_type=MESH)
    for offset in range(1, bands):
        pl.semaphore_signal(barrier, inc=1, device_id=(ka, (band + offset) % bands), device_id_type=MESH)

    def dot(a, b):
        return jnp.dot(a, b, preferred_element_type=f32)

    def iotas(shape):
        return (lax.broadcasted_iota(jnp.int32, shape, 0), lax.broadcasted_iota(jnp.int32, shape, 1))

    slots[0, :, padded - LANES:] = jnp.zeros((2 * width, LANES), bf16)
    r, c = iotas((2 * width, occupied))
    c = c - band * width
    pick_re = jnp.where((c >= 0) & (c < width) & (c == r), 1.0, 0.0).astype(bf16)
    pick_im = jnp.where((c >= 0) & (c < width) & (c == r - width), 1.0, 0.0).astype(bf16)
    fetches[0].wait()
    re, im = own[0, 0], own[0, 1]
    slots[0, :, :functions] = (dot(pick_re, re) + dot(pick_im, im)).astype(bf16)

    pl.semaphore_wait(barrier, 2 + 1 + bands - 1)

    def ring_copy(to_right, s, h):
        if to_right:
            src, dst, ss, rs, to = jnp.maximum(2 * s - 3, 0), 2 * s - 1, right_s, right_r, member(1)
        else:
            dst = jnp.where(s == half, n - 1, 2 * s)
            src, ss, rs, to = 2 * s - 2, left_s, left_r, member(-1)
        return pltpu.make_async_remote_copy(
            src_ref=slots.at[src, :, chunks[h]], dst_ref=slots.at[dst, :, chunks[h]],
            send_sem=ss.at[s - 1, h], recv_sem=rs.at[s - 1, h],
            device_id=(to, band), device_id_type=MESH)

    def steps(to_right, h):
        return half if h == (0 if to_right else 1) else half - 1

    start = pl.multiple_of(jnp.minimum(chip * 2 * columns // LANES, tiles - window // LANES) * LANES, LANES)

    def window_copy(g, t):
        return pltpu.make_async_remote_copy(
            src_ref=slots.at[t, :, pl.ds(start, window)], dst_ref=near.at[g - 1, t],
            send_sem=win_s.at[g - 1, t], recv_sem=win_r.at[g - 1, t],
            device_id=(ka, (band + g) % bands), device_id_type=MESH)

    def spread(t):
        for g in range(1, bands):
            window_copy(g, t).start()

    for h in range(2):
        for side in (True, False):
            ring_copy(side, 1, h).start()
    spread(0)

    r, c = iotas((occupied, lanes))
    hits = [jnp.zeros(r.shape, f32), jnp.zeros(r.shape, f32)]
    for ri in range(2):
        for g in range(bands):
            low = (ri * bands + g) * STRIDE
            inside = (c >= low) & (c < low + width)
            hits[ri] = jnp.where(inside & (r - ((band - g + bands) % bands) * width == c - low), 1.0, hits[ri])
    mine = pl.ds(pl.multiple_of(core * lanes, LANES), lanes)
    sel[padded - LANES:, mine] = jnp.zeros((LANES, lanes), bf16)

    def turned(value, hit):
        return lax.dot_general(value, hit.astype(bf16), (((0,), (0,)), ((), ())), preferred_element_type=f32)

    sel[:functions, mine] = (turned(re, hits[0]) + turned(im, hits[1])).astype(bf16)
    sel_copy = pltpu.make_async_remote_copy(
        src_ref=sel.at[:, mine], dst_ref=sel.at[:, mine], send_sem=one_s.at[0], recv_sem=one_r.at[0],
        device_id=(sibling, band), device_id_type=MESH)
    sel_copy.start()
    for fetch in fetches[1:]:
        fetch.wait()

    at = lax.broadcasted_iota(jnp.int32, (n, 2 * lanes), 0)
    where = wrap(jnp.where(at % 2 == 0, ring + at // 2, ring - at // 2 - 1))
    kpoint = (2 * chip_at(where) + core).astype(f32)
    lane = lax.broadcasted_iota(jnp.int32, (n, 2 * lanes), 1)
    sign = jnp.where(lane % lanes < lanes // 2, 1.0, -1.0)
    for f in range(cells):
        turns = kpoint * (frag[f].astype(f32) / nk)
        angle = 2.0 * math.pi * (turns - jnp.floor(turns))
        turn[f] = jnp.cos(angle) / nk
        turn[cells + f] = sign * jnp.sin(angle) / nk
    def swap(x):
        return pltpu.roll(x, lanes // 2, 1)

    def swap_both(x):
        return jnp.concatenate([swap(x[:, :lanes]), swap(x[:, lanes:])], 1)

    own_lane = lax.broadcasted_iota(jnp.int32, (width, 2 * lanes), 1)
    signs = jnp.where(own_lane % lanes < lanes // 2, 1.0, -1.0)

    def product_of(i, h):
        return dot(slots[pl.ds(2 * i, 2), :, chunks[h]].reshape(4 * width, -1), sel[chunks[h], :])

    def overlap(i, product):
        for side in range(2):
            low = 2 * width * side
            k = 2 * chip_at(wrap(ring - i - 1 if side else ring + i)) + core
            value = product[low:low + width] + signs * swap_both(product[low + width:low + 2 * width])
            scale = jnp.where(own_lane < lanes, weight[classes[k, 2 * chip]], weight[classes[k, 2 * chip + 1]])
            value = (scale / functions * value).astype(bf16).astype(f32)
            other = swap_both(value)
            at = pl.ds(2 * i + side, 1)
            acc[...] += jnp.concatenate(
                [turn[f, at, :] * value + turn[cells + f, at, :] * other for f in range(cells)], 0)

    r, c = iotas((lanes, 2 * width))
    placers = []
    for g in range(bands):
        a, b = g * STRIDE, (bands + g) * STRIDE
        hit = ((c < width) & (r == a + c)) | ((c >= width) & (r == b + c - width))
        placers.append(jnp.where(hit, 1.0, 0.0).astype(bf16))

    offset = chip * 2 * columns - start

    def place(t):
        value = dot(placers[0], slots[t, :, pl.ds(start, window)])
        for g in range(1, bands):
            window_copy(g, t).wait_recv()
            value = value + dot(placers[g], near[g - 1, t])
        for c in range(2):
            stack[c, t] = pltpu.roll(value, window - offset - (core if c else 1 - core) * columns, 1)[:, :wide].astype(bf16)

    acc[...] = jnp.zeros((rows, 2 * lanes), f32)

    @pl.loop(0, half)
    def _(i):
        s = i + 1
        for h in range(2):
            for side in (True, False):
                last = steps(side, h)

                @pl.when(s <= last)
                def _():
                    ring_copy(side, s, h).wait_recv()

                @pl.when(s < last)
                def _():
                    ring_copy(side, s + 1, h).start()
            if h == 0:
                @pl.when(i == 0)
                def _():
                    sel_copy.wait()

                product = product_of(i, 0)
        spread(2 * s - 1)

        @pl.when(s < half)
        def _():
            spread(2 * s)

        overlap(i, product + product_of(i, 1))

        @pl.when(i > 0)
        def _():
            place(2 * i - 2)
            place(2 * i - 1)

    theirs = pl.ds(pl.multiple_of((1 - core) * lanes, LANES), lanes)
    acc_copy = pltpu.make_async_remote_copy(
        src_ref=acc.at[:, theirs], dst_ref=acc_in, send_sem=one_s.at[1], recv_sem=one_r.at[1],
        device_id=(sibling, band), device_id_type=MESH)
    acc_copy.start()
    acc_copy.wait_recv()
    packed[0] = acc[:, mine] + acc_in[...]

    def place_at(receiver, source):
        t = wrap(receiver - source)
        return jnp.where((t > 0) & (t <= half), 2 * t - 1, jnp.where(t == 0, 0, 2 * (n - t)))

    def ring_of(line, side):
        return jnp.where(side == 0, line, n - 1 - line)

    def line_at(d):
        line = jnp.where(row + d >= half, row + d - half, row + d)
        return jnp.where(line < 0, line + half, line)

    def gather_copy(d):
        line = line_at(d)
        return pltpu.make_async_remote_copy(
            src_ref=packed.at[0], dst_ref=packed.at[place_at(ring_of(line, odd), ring)],
            send_sem=gat_s.at[d - 1], recv_sem=gat_r.at[d - 1],
            device_id=(2 * (2 * line + odd) + core, band), device_id_type=MESH)

    def across_copy(d):
        source = ring_of(line_at(-d), odd)
        return pltpu.make_async_remote_copy(
            src_ref=packed.at[place_at(ring, source)], dst_ref=packed.at[place_at(n - 1 - ring, source)],
            send_sem=gat_s.at[half - 1 + d], recv_sem=gat_r.at[half - 1 + d],
            device_id=(2 * (chip + 1 - 2 * odd) + core, band), device_id_type=MESH)

    across_copy(0).start()
    for d in range(1, half):
        gather_copy(d).start()
    for d in range(1, half):
        gather_copy(d).wait_recv()
        across_copy(d).start()
    place(n - 2)
    place(n - 1)

    column = lax.broadcasted_iota(jnp.int32, (width, wide), 1) + ka * columns
    block = functions // blocks
    masks = []
    for f in range(cells):
        mask = jnp.zeros((width, wide), f32)
        for i in range(blocks):
            keep = (column >= i * block) & (column < (i + 1) * block)
            mask = jnp.where(keep, pattern[f, i].astype(f32), mask)
        masks.append(mask)

    @pl.loop(1, half + 1)
    def _(s):
        for h in range(2):
            for side in (True, False):
                @pl.when(s <= steps(side, h))
                def _():
                    ring_copy(side, s, h).wait_send()

    @pl.loop(0, n)
    def _(t):
        for g in range(1, bands):
            window_copy(g, t).wait_send()

    acc_copy.wait_send()
    for d in range(half):
        across_copy(d).wait_recv()

    rotated = lax.broadcasted_iota(jnp.int32, (rows, lanes), 1)
    flip = jnp.where(rotated < lanes // 2, -1.0, 1.0)
    real = [packed[t] for t in range(n)]
    left = jnp.concatenate(
        [jnp.concatenate(real, 1), jnp.concatenate([flip * swap(x) for x in real], 1)], 0)
    high = left.astype(bf16)
    low = (left - high.astype(f32)).astype(bf16)
    factors = jnp.concatenate([high, low], 0)

    def part_of(c):
        value = dot(factors, stack[c].reshape(n * lanes, wide))
        return value[:2 * rows] + value[2 * rows:]

    part[...] = part_of(0)
    part_copy = pltpu.make_async_remote_copy(
        src_ref=part, dst_ref=part_in, send_sem=one_s.at[2], recv_sem=one_r.at[2],
        device_id=(sibling, band), device_id_type=MESH)
    part_copy.start()
    kept = part_of(1)
    part_copy.wait_recv()
    whole = kept + part_in[...]
    for ri in range(2):
        for f in range(cells):
            spot = (ri * cells + f) * width
            out[f, ri] = (whole[spot:spot + width] * masks[f])[:, :columns]

    for d in range(1, half):
        gather_copy(d).wait_send()
    for d in range(half):
        across_copy(d).wait_send()
    part_copy.wait_send()


def solution(mesh):
    nk, bands = mesh.shape["ka"], mesh.shape["band"]
    n = nk // 2

    def shards(coefficients, class_weight, diff_class, frag_cells, block_pattern):
        occupied, functions = coefficients.shape[2:]
        width = occupied // bands
        cells, blocks = block_pattern.shape
        padded = (functions + LANES - 1) // LANES * LANES
        columns = functions // nk
        window = (2 * columns + 2 * LANES - 2) // LANES * LANES
        wide = (columns + LANES - 1) // LANES * LANES
        lanes = 2 * bands * STRIDE
        rows = cells * width
        hbm = pl.BlockSpec(memory_space=pltpu.HBM)
        bf16, f32 = jnp.bfloat16, jnp.float32
        dma = pltpu.SemaphoreType.DMA
        operands = (coefficients, class_weight, diff_class, frag_cells, block_pattern)
        return pl.pallas_call(
            functools.partial(kernel, nk, bands, width, occupied, functions, blocks, cells),
            out_shape=jax.ShapeDtypeStruct((cells, 2, width, columns), f32),
            in_specs=[hbm] * 5,
            out_specs=pl.BlockSpec(memory_space=pltpu.VMEM),
            scratch_shapes=[
                pltpu.VMEM(coefficients.shape, bf16),
                *[pltpu.SMEM(x.shape, x.dtype) for x in operands[1:]],
                pltpu.VMEM((padded, 2 * lanes), bf16),
                pltpu.VMEM((n, 2 * width, padded), bf16),
                pltpu.VMEM((bands - 1, n, 2 * width, window), bf16),
                pltpu.VMEM((2, n, lanes, wide), bf16),
                pltpu.VMEM((2 * cells, n, 2 * lanes), f32),
                pltpu.VMEM((rows, 2 * lanes), f32),
                pltpu.VMEM((rows, lanes), f32),
                pltpu.VMEM((n, rows, lanes), f32),
                pltpu.VMEM((2 * rows, wide), f32),
                pltpu.VMEM((2 * rows, wide), f32),
                dma((5,)),
                dma((n // 2, 2)), dma((n // 2, 2)), dma((n // 2, 2)), dma((n // 2, 2)),
                dma((bands - 1, n)), dma((bands - 1, n)),
                dma((n - 1,)), dma((n - 1,)), dma((3,)), dma((3,)),
            ],
            compiler_params=pltpu.CompilerParams(
                collective_id=0, has_side_effects=True, vmem_limit_bytes=63 * 2**20),
            cost_estimate=pl.CostEstimate(
                flops=8 * n * width * lanes * padded, bytes_accessed=8 * n * width * padded, transcendentals=0),
            name="exchange",
        )(*operands)

    placed = (P("ka", None, None, None), P(), P(), P(), P())
    return jax.shard_map(
        shards, mesh=mesh, in_specs=placed, out_specs=P(None, None, "band", "ka"), check_vma=False)
```

```python
import functools
import math

import jax
import jax.numpy as jnp
from jax import lax
from jax.experimental import pallas as pl
from jax.experimental.pallas import tpu as pltpu
from jax.sharding import PartitionSpec as P

MESH = pl.DeviceIdType.MESH
LANES = 128
CHUNKS = 4
STRIDE = 32


def kernel(nk, bands, width, occupied, functions, blocks, cells,
           own_hbm, weight_hbm, classes_hbm, frag_hbm, pattern_hbm, out,
           own, weight, classes, frag, pattern,
           sel, slots, near, stack, turn, acc, acc_in, packed, part, part_in,
           in_s, right_s, right_r, left_s, left_r, win_s, win_r, gat_s, gat_r, one_s, one_r):
    n = nk // 2
    half = n // 2
    ka, band = lax.axis_index("ka"), lax.axis_index("band")
    chip, core = ka // 2, ka % 2
    padded = slots.shape[2]
    tiles = padded // LANES
    ends = [(tiles * h + CHUNKS - 1) // CHUNKS * LANES for h in range(CHUNKS + 1)]
    chunks = [pl.ds(ends[h], ends[h + 1] - ends[h]) for h in range(CHUNKS)]
    middle = ends[CHUNKS // 2]
    halves = (pl.ds(0, middle), pl.ds(middle, padded - middle))
    window, wide = near.shape[3], stack.shape[3]
    columns = functions // nk
    lanes = 2 * bands * STRIDE
    rows = cells * width
    f32, bf16 = jnp.float32, jnp.bfloat16

    operands = (own_hbm, weight_hbm, classes_hbm, frag_hbm, pattern_hbm)
    fetches = [pltpu.make_async_copy(src, dst, in_s.at[i])
               for i, (src, dst) in enumerate(zip(operands, (own, weight, classes, frag, pattern)))]
    for fetch in fetches:
        fetch.start()

    def chip_at(ring):
        return jnp.where(ring < half, 2 * ring, 2 * (n - 1 - ring) + 1)

    row, odd = chip // 2, chip % 2
    ring = jnp.where(odd == 0, row, n - 1 - row)

    def wrap(x):
        x = jnp.where(x >= n, x - n, x)
        return jnp.where(x < 0, x + n, x)

    members = [2 * chip_at(wrap(ring + offset)) + core for offset in range(n)]

    def member(offset):
        return members[offset % n]

    sibling = 2 * chip + 1 - core
    barrier = pltpu.get_barrier_semaphore()
    for offset in (1, -1):
        pl.semaphore_signal(barrier, inc=1, device_id=(member(offset), band), device_id_type=MESH)
    pl.semaphore_signal(barrier, inc=1, device_id=(sibling, band), device_id_type=MESH)
    for offset in range(1, bands):
        pl.semaphore_signal(barrier, inc=1, device_id=(ka, (band + offset) % bands), device_id_type=MESH)

    def dot(a, b):
        return jnp.dot(a, b, preferred_element_type=f32)

    def iotas(shape):
        return (lax.broadcasted_iota(jnp.int32, shape, 0), lax.broadcasted_iota(jnp.int32, shape, 1))

    slots[0, :, padded - LANES:] = jnp.zeros((2 * width, LANES), bf16)
    r, c = iotas((2 * width, occupied))
    c = c - band * width
    pick_re = jnp.where((c >= 0) & (c < width) & (c == r), 1.0, 0.0).astype(bf16)
    pick_im = jnp.where((c >= 0) & (c < width) & (c == r - width), 1.0, 0.0).astype(bf16)
    fetches[0].wait()
    re, im = own[0, 0], own[0, 1]
    slots[0, :, :functions] = (dot(pick_re, re) + dot(pick_im, im)).astype(bf16)

    pl.semaphore_wait(barrier, 2 + 1 + bands - 1)

    def ring_copy(to_right, s, h):
        if to_right:
            src, dst, ss, rs, to = jnp.maximum(2 * s - 3, 0), 2 * s - 1, right_s, right_r, member(1)
        else:
            dst = jnp.where(s == half, n - 1, 2 * s)
            src, ss, rs, to = 2 * s - 2, left_s, left_r, member(-1)
        return pltpu.make_async_remote_copy(
            src_ref=slots.at[src, :, chunks[h]], dst_ref=slots.at[dst, :, chunks[h]],
            send_sem=ss.at[s - 1, h], recv_sem=rs.at[s - 1, h],
            device_id=(to, band), device_id_type=MESH)

    def turn_of(to_right, h):
        return h if to_right else (h + CHUNKS // 2) % CHUNKS

    def steps(to_right, h):
        return half if (h < CHUNKS // 2) == to_right else half - 1

    start = pl.multiple_of(jnp.minimum(chip * 2 * columns // LANES, tiles - window // LANES) * LANES, LANES)

    def window_copy(g, t):
        return pltpu.make_async_remote_copy(
            src_ref=slots.at[t, :, pl.ds(start, window)], dst_ref=near.at[g - 1, t],
            send_sem=win_s.at[g - 1, t], recv_sem=win_r.at[g - 1, t],
            device_id=(ka, (band + g) % bands), device_id_type=MESH)

    def spread(t):
        for g in range(1, bands):
            window_copy(g, t).start()

    for h in range(CHUNKS):
        for side in (True, False):
            ring_copy(side, 1, turn_of(side, h)).start()
    spread(0)

    r, c = iotas((occupied, lanes))
    hits = [jnp.zeros(r.shape, f32), jnp.zeros(r.shape, f32)]
    for ri in range(2):
        for g in range(bands):
            low = (ri * bands + g) * STRIDE
            inside = (c >= low) & (c < low + width)
            hits[ri] = jnp.where(inside & (r - ((band - g + bands) % bands) * width == c - low), 1.0, hits[ri])
    mine = pl.ds(pl.multiple_of(core * lanes, LANES), lanes)
    sel[padded - LANES:, mine] = jnp.zeros((LANES, lanes), bf16)

    def turned(value, hit):
        return lax.dot_general(value, hit.astype(bf16), (((0,), (0,)), ((), ())), preferred_element_type=f32)

    sel[:functions, mine] = (turned(re, hits[0]) + turned(im, hits[1])).astype(bf16)
    sel_copy = pltpu.make_async_remote_copy(
        src_ref=sel.at[:, mine], dst_ref=sel.at[:, mine], send_sem=one_s.at[0], recv_sem=one_r.at[0],
        device_id=(sibling, band), device_id_type=MESH)
    sel_copy.start()
    for fetch in fetches[1:]:
        fetch.wait()

    at = lax.broadcasted_iota(jnp.int32, (n, 2 * lanes), 0)
    where = wrap(jnp.where(at % 2 == 0, ring + at // 2, ring - at // 2 - 1))
    kpoint = (2 * chip_at(where) + core).astype(f32)
    lane = lax.broadcasted_iota(jnp.int32, (n, 2 * lanes), 1)
    sign = jnp.where(lane % lanes < lanes // 2, 1.0, -1.0)
    for f in range(cells):
        turns = kpoint * (frag[f].astype(f32) / nk)
        angle = 2.0 * math.pi * (turns - jnp.floor(turns))
        turn[f] = jnp.cos(angle) / nk
        turn[cells + f] = sign * jnp.sin(angle) / nk
    def swap(x):
        return pltpu.roll(x, lanes // 2, 1)

    def swap_both(x):
        return jnp.concatenate([swap(x[:, :lanes]), swap(x[:, lanes:])], 1)

    own_lane = lax.broadcasted_iota(jnp.int32, (width, 2 * lanes), 1)
    signs = jnp.where(own_lane % lanes < lanes // 2, 1.0, -1.0)

    def product_of(i, h):
        return dot(slots[pl.ds(2 * i, 2), :, halves[h]].reshape(4 * width, -1), sel[halves[h], :])

    def overlap(i, product):
        for side in range(2):
            low = 2 * width * side
            k = 2 * chip_at(wrap(ring - i - 1 if side else ring + i)) + core
            value = product[low:low + width] + signs * swap_both(product[low + width:low + 2 * width])
            scale = jnp.where(own_lane < lanes, weight[classes[k, 2 * chip]], weight[classes[k, 2 * chip + 1]])
            value = (scale / functions * value).astype(bf16).astype(f32)
            other = swap_both(value)
            at = pl.ds(2 * i + side, 1)
            acc[...] += jnp.concatenate(
                [turn[f, at, :] * value + turn[cells + f, at, :] * other for f in range(cells)], 0)

    r, c = iotas((lanes, 2 * width))
    placers = []
    for g in range(bands):
        a, b = g * STRIDE, (bands + g) * STRIDE
        hit = ((c < width) & (r == a + c)) | ((c >= width) & (r == b + c - width))
        placers.append(jnp.where(hit, 1.0, 0.0).astype(bf16))

    offset = chip * 2 * columns - start

    def place(t):
        value = dot(placers[0], slots[t, :, pl.ds(start, window)])
        for g in range(1, bands):
            window_copy(g, t).wait_recv()
            value = value + dot(placers[g], near[g - 1, t])
        for c in range(2):
            stack[c, t] = pltpu.roll(value, window - offset - (core if c else 1 - core) * columns, 1)[:, :wide].astype(bf16)

    acc[...] = jnp.zeros((rows, 2 * lanes), f32)

    @pl.loop(0, half)
    def _(i):
        s = i + 1
        for h in range(CHUNKS):
            for side in (True, False):
                chunk = turn_of(side, h)
                last = steps(side, chunk)

                @pl.when(s <= last)
                def _():
                    ring_copy(side, s, chunk).wait_recv()

                @pl.when(s < last)
                def _():
                    ring_copy(side, s + 1, chunk).start()
            if h == CHUNKS // 2 - 1:
                @pl.when(i == 0)
                def _():
                    sel_copy.wait()

                product = product_of(i, 0)
        spread(2 * s - 1)

        @pl.when(s < half)
        def _():
            spread(2 * s)

        overlap(i, product + product_of(i, 1))

        @pl.when(i > 0)
        def _():
            place(2 * i - 2)
            place(2 * i - 1)

    theirs = pl.ds(pl.multiple_of((1 - core) * lanes, LANES), lanes)
    acc_copy = pltpu.make_async_remote_copy(
        src_ref=acc.at[:, theirs], dst_ref=acc_in, send_sem=one_s.at[1], recv_sem=one_r.at[1],
        device_id=(sibling, band), device_id_type=MESH)
    acc_copy.start()
    acc_copy.wait_recv()
    packed[0] = acc[:, mine] + acc_in[...]

    def place_of(t):
        return 2 * t - 1 if 0 < t <= half else 2 * ((n - t) % n)

    def gather_copy(t):
        return pltpu.make_async_remote_copy(
            src_ref=packed.at[0], dst_ref=packed.at[place_of(t)], send_sem=gat_s.at[t - 1], recv_sem=gat_r.at[t - 1],
            device_id=(member(t), band), device_id_type=MESH)

    order = sorted(range(1, n), key=lambda t: -min(t, n - t))
    for t in order:
        gather_copy(t).start()
    place(n - 2)
    place(n - 1)

    column = lax.broadcasted_iota(jnp.int32, (width, wide), 1) + ka * columns
    block = functions // blocks
    masks = []
    for f in range(cells):
        mask = jnp.zeros((width, wide), f32)
        for i in range(blocks):
            keep = (column >= i * block) & (column < (i + 1) * block)
            mask = jnp.where(keep, pattern[f, i].astype(f32), mask)
        masks.append(mask)

    @pl.loop(1, half + 1)
    def _(s):
        for h in range(CHUNKS):
            for side in (True, False):
                @pl.when(s <= steps(side, h))
                def _():
                    ring_copy(side, s, h).wait_send()

    @pl.loop(0, n)
    def _(t):
        for g in range(1, bands):
            window_copy(g, t).wait_send()

    acc_copy.wait_send()
    for t in order:
        gather_copy(t).wait_recv()

    rotated = lax.broadcasted_iota(jnp.int32, (rows, lanes), 1)
    flip = jnp.where(rotated < lanes // 2, -1.0, 1.0)
    real = [packed[t] for t in range(n)]
    left = jnp.concatenate(
        [jnp.concatenate(real, 1), jnp.concatenate([flip * swap(x) for x in real], 1)], 0)
    high = left.astype(bf16)
    low = (left - high.astype(f32)).astype(bf16)
    factors = jnp.concatenate([high, low], 0)

    def part_of(c):
        value = dot(factors, stack[c].reshape(n * lanes, wide))
        return value[:2 * rows] + value[2 * rows:]

    part[...] = part_of(0)
    part_copy = pltpu.make_async_remote_copy(
        src_ref=part, dst_ref=part_in, send_sem=one_s.at[2], recv_sem=one_r.at[2],
        device_id=(sibling, band), device_id_type=MESH)
    part_copy.start()
    kept = part_of(1)
    part_copy.wait_recv()
    whole = kept + part_in[...]
    for ri in range(2):
        for f in range(cells):
            spot = (ri * cells + f) * width
            out[f, ri] = (whole[spot:spot + width] * masks[f])[:, :columns]

    for t in order:
        gather_copy(t).wait_send()
    part_copy.wait_send()


def solution(mesh):
    nk, bands = mesh.shape["ka"], mesh.shape["band"]
    n = nk // 2

    def shards(coefficients, class_weight, diff_class, frag_cells, block_pattern):
        occupied, functions = coefficients.shape[2:]
        width = occupied // bands
        cells, blocks = block_pattern.shape
        padded = (functions + LANES - 1) // LANES * LANES
        columns = functions // nk
        window = (2 * columns + 2 * LANES - 2) // LANES * LANES
        wide = (columns + LANES - 1) // LANES * LANES
        lanes = 2 * bands * STRIDE
        rows = cells * width
        hbm = pl.BlockSpec(memory_space=pltpu.HBM)
        bf16, f32 = jnp.bfloat16, jnp.float32
        dma = pltpu.SemaphoreType.DMA
        operands = (coefficients, class_weight, diff_class, frag_cells, block_pattern)
        return pl.pallas_call(
            functools.partial(kernel, nk, bands, width, occupied, functions, blocks, cells),
            out_shape=jax.ShapeDtypeStruct((cells, 2, width, columns), f32),
            in_specs=[hbm] * 5,
            out_specs=pl.BlockSpec(memory_space=pltpu.VMEM),
            scratch_shapes=[
                pltpu.VMEM(coefficients.shape, bf16),
                *[pltpu.SMEM(x.shape, x.dtype) for x in operands[1:]],
                pltpu.VMEM((padded, 2 * lanes), bf16),
                pltpu.VMEM((n, 2 * width, padded), bf16),
                pltpu.VMEM((bands - 1, n, 2 * width, window), bf16),
                pltpu.VMEM((2, n, lanes, wide), bf16),
                pltpu.VMEM((2 * cells, n, 2 * lanes), f32),
                pltpu.VMEM((rows, 2 * lanes), f32),
                pltpu.VMEM((rows, lanes), f32),
                pltpu.VMEM((n, rows, lanes), f32),
                pltpu.VMEM((2 * rows, wide), f32),
                pltpu.VMEM((2 * rows, wide), f32),
                dma((5,)),
                *[dma((n // 2, CHUNKS))] * 4,
                dma((bands - 1, n)), dma((bands - 1, n)),
                dma((n - 1,)), dma((n - 1,)), dma((3,)), dma((3,)),
            ],
            compiler_params=pltpu.CompilerParams(
                collective_id=0, has_side_effects=True, vmem_limit_bytes=63 * 2**20),
            cost_estimate=pl.CostEstimate(
                flops=8 * n * width * lanes * padded, bytes_accessed=8 * n * width * padded, transcendentals=0),
            name="exchange",
        )(*operands)

    placed = (P("ka", None, None, None), P(), P(), P(), P())
    return jax.shard_map(
        shards, mesh=mesh, in_specs=placed, out_specs=P(None, None, "band", "ka"), check_vma=False)
```

```python
import functools
import math

import jax
import jax.numpy as jnp
from jax import lax
from jax.experimental import pallas as pl
from jax.experimental.pallas import tpu as pltpu
from jax.sharding import PartitionSpec as P

MESH = pl.DeviceIdType.MESH
LANES = 128
CHUNKS = 6
STRIDE = 32


def kernel(nk, bands, width, occupied, functions, blocks, cells,
           own_hbm, weight_hbm, classes_hbm, frag_hbm, pattern_hbm, out,
           own, weight, classes, frag, pattern,
           sel, slots, near, stack, turn, acc, acc_in, packed, part, part_in,
           in_s, right_s, right_r, left_s, left_r, win_s, win_r, gat_s, gat_r, one_s, one_r):
    n = nk // 2
    half = n // 2
    ka, band = lax.axis_index("ka"), lax.axis_index("band")
    chip, core = ka // 2, ka % 2
    padded = slots.shape[2]
    tiles = padded // LANES
    ends = [(tiles * h + CHUNKS - 1) // CHUNKS * LANES for h in range(CHUNKS + 1)]
    chunks = [pl.ds(ends[h], ends[h + 1] - ends[h]) for h in range(CHUNKS)]
    middle = ends[CHUNKS // 2]
    halves = (pl.ds(0, middle), pl.ds(middle, padded - middle))
    window, wide = near.shape[3], stack.shape[3]
    columns = functions // nk
    lanes = 2 * bands * STRIDE
    rows = cells * width
    f32, bf16 = jnp.float32, jnp.bfloat16

    operands = (own_hbm, weight_hbm, classes_hbm, frag_hbm, pattern_hbm)
    fetches = [pltpu.make_async_copy(src, dst, in_s.at[i])
               for i, (src, dst) in enumerate(zip(operands, (own, weight, classes, frag, pattern)))]
    for fetch in fetches:
        fetch.start()

    def chip_at(ring):
        return jnp.where(ring < half, 2 * ring, 2 * (n - 1 - ring) + 1)

    row, odd = chip // 2, chip % 2
    ring = jnp.where(odd == 0, row, n - 1 - row)

    def wrap(x):
        x = jnp.where(x >= n, x - n, x)
        return jnp.where(x < 0, x + n, x)

    members = [2 * chip_at(wrap(ring + offset)) + core for offset in range(n)]

    def member(offset):
        return members[offset % n]

    sibling = 2 * chip + 1 - core
    barrier = pltpu.get_barrier_semaphore()
    for offset in (1, -1):
        pl.semaphore_signal(barrier, inc=1, device_id=(member(offset), band), device_id_type=MESH)
    pl.semaphore_signal(barrier, inc=1, device_id=(sibling, band), device_id_type=MESH)
    for offset in range(1, bands):
        pl.semaphore_signal(barrier, inc=1, device_id=(ka, (band + offset) % bands), device_id_type=MESH)

    def dot(a, b):
        return jnp.dot(a, b, preferred_element_type=f32)

    def iotas(shape):
        return (lax.broadcasted_iota(jnp.int32, shape, 0), lax.broadcasted_iota(jnp.int32, shape, 1))

    slots[0, :, padded - LANES:] = jnp.zeros((2 * width, LANES), bf16)
    r, c = iotas((2 * width, occupied))
    c = c - band * width
    pick_re = jnp.where((c >= 0) & (c < width) & (c == r), 1.0, 0.0).astype(bf16)
    pick_im = jnp.where((c >= 0) & (c < width) & (c == r - width), 1.0, 0.0).astype(bf16)
    fetches[0].wait()
    re, im = own[0, 0], own[0, 1]
    slots[0, :, :functions] = (dot(pick_re, re) + dot(pick_im, im)).astype(bf16)

    pl.semaphore_wait(barrier, 2 + 1 + bands - 1)

    def ring_copy(to_right, s, h):
        if to_right:
            src, dst, ss, rs, to = jnp.maximum(2 * s - 3, 0), 2 * s - 1, right_s, right_r, member(1)
        else:
            dst = jnp.where(s == half, n - 1, 2 * s)
            src, ss, rs, to = 2 * s - 2, left_s, left_r, member(-1)
        return pltpu.make_async_remote_copy(
            src_ref=slots.at[src, :, chunks[h]], dst_ref=slots.at[dst, :, chunks[h]],
            send_sem=ss.at[s - 1, h], recv_sem=rs.at[s - 1, h],
            device_id=(to, band), device_id_type=MESH)

    def turn_of(to_right, h):
        return h if to_right else (h + CHUNKS // 2) % CHUNKS

    def steps(to_right, h):
        return half if (h < CHUNKS // 2) == to_right else half - 1

    start = pl.multiple_of(jnp.minimum(chip * 2 * columns // LANES, tiles - window // LANES) * LANES, LANES)

    def window_copy(g, t):
        return pltpu.make_async_remote_copy(
            src_ref=slots.at[t, :, pl.ds(start, window)], dst_ref=near.at[g - 1, t],
            send_sem=win_s.at[g - 1, t], recv_sem=win_r.at[g - 1, t],
            device_id=(ka, (band + g) % bands), device_id_type=MESH)

    def spread(t):
        for g in range(1, bands):
            window_copy(g, t).start()

    for h in range(CHUNKS):
        for side in (True, False):
            ring_copy(side, 1, turn_of(side, h)).start()
    spread(0)

    r, c = iotas((occupied, lanes))
    hits = [jnp.zeros(r.shape, f32), jnp.zeros(r.shape, f32)]
    for ri in range(2):
        for g in range(bands):
            low = (ri * bands + g) * STRIDE
            inside = (c >= low) & (c < low + width)
            hits[ri] = jnp.where(inside & (r - ((band - g + bands) % bands) * width == c - low), 1.0, hits[ri])
    mine = pl.ds(pl.multiple_of(core * lanes, LANES), lanes)
    sel[padded - LANES:, mine] = jnp.zeros((LANES, lanes), bf16)

    def turned(value, hit):
        return lax.dot_general(value, hit.astype(bf16), (((0,), (0,)), ((), ())), preferred_element_type=f32)

    sel[:functions, mine] = (turned(re, hits[0]) + turned(im, hits[1])).astype(bf16)
    sel_copy = pltpu.make_async_remote_copy(
        src_ref=sel.at[:, mine], dst_ref=sel.at[:, mine], send_sem=one_s.at[0], recv_sem=one_r.at[0],
        device_id=(sibling, band), device_id_type=MESH)
    sel_copy.start()
    for fetch in fetches[1:]:
        fetch.wait()

    at = lax.broadcasted_iota(jnp.int32, (n, 2 * lanes), 0)
    where = wrap(jnp.where(at % 2 == 0, ring + at // 2, ring - at // 2 - 1))
    kpoint = (2 * chip_at(where) + core).astype(f32)
    lane = lax.broadcasted_iota(jnp.int32, (n, 2 * lanes), 1)
    sign = jnp.where(lane % lanes < lanes // 2, 1.0, -1.0)
    for f in range(cells):
        turns = kpoint * (frag[f].astype(f32) / nk)
        angle = 2.0 * math.pi * (turns - jnp.floor(turns))
        turn[f] = jnp.cos(angle) / nk
        turn[cells + f] = sign * jnp.sin(angle) / nk
    def swap(x):
        return pltpu.roll(x, lanes // 2, 1)

    def swap_both(x):
        return jnp.concatenate([swap(x[:, :lanes]), swap(x[:, lanes:])], 1)

    own_lane = lax.broadcasted_iota(jnp.int32, (width, 2 * lanes), 1)
    signs = jnp.where(own_lane % lanes < lanes // 2, 1.0, -1.0)

    def product_of(i, h):
        return dot(slots[pl.ds(2 * i, 2), :, halves[h]].reshape(4 * width, -1), sel[halves[h], :])

    def overlap(i, product):
        for side in range(2):
            low = 2 * width * side
            k = 2 * chip_at(wrap(ring - i - 1 if side else ring + i)) + core
            value = product[low:low + width] + signs * swap_both(product[low + width:low + 2 * width])
            scale = jnp.where(own_lane < lanes, weight[classes[k, 2 * chip]], weight[classes[k, 2 * chip + 1]])
            value = (scale / functions * value).astype(bf16).astype(f32)
            other = swap_both(value)
            at = pl.ds(2 * i + side, 1)
            acc[...] += jnp.concatenate(
                [turn[f, at, :] * value + turn[cells + f, at, :] * other for f in range(cells)], 0)

    r, c = iotas((lanes, 2 * width))
    placers = []
    for g in range(bands):
        a, b = g * STRIDE, (bands + g) * STRIDE
        hit = ((c < width) & (r == a + c)) | ((c >= width) & (r == b + c - width))
        placers.append(jnp.where(hit, 1.0, 0.0).astype(bf16))

    offset = chip * 2 * columns - start

    def place(t):
        value = dot(placers[0], slots[t, :, pl.ds(start, window)])
        for g in range(1, bands):
            window_copy(g, t).wait_recv()
            value = value + dot(placers[g], near[g - 1, t])
        for c in range(2):
            stack[c, t] = pltpu.roll(value, window - offset - (core if c else 1 - core) * columns, 1)[:, :wide].astype(bf16)

    acc[...] = jnp.zeros((rows, 2 * lanes), f32)

    @pl.loop(0, half)
    def _(i):
        s = i + 1
        for h in range(CHUNKS):
            for side in (True, False):
                chunk = turn_of(side, h)
                last = steps(side, chunk)

                @pl.when(s <= last)
                def _():
                    ring_copy(side, s, chunk).wait_recv()

                @pl.when(s < last)
                def _():
                    ring_copy(side, s + 1, chunk).start()
            if h == CHUNKS // 2 - 1:
                @pl.when(i == 0)
                def _():
                    sel_copy.wait()

                product = product_of(i, 0)
        spread(2 * s - 1)

        @pl.when(s < half)
        def _():
            spread(2 * s)

        overlap(i, product + product_of(i, 1))

        @pl.when(i > 0)
        def _():
            place(2 * i - 2)
            place(2 * i - 1)

    theirs = pl.ds(pl.multiple_of((1 - core) * lanes, LANES), lanes)
    acc_copy = pltpu.make_async_remote_copy(
        src_ref=acc.at[:, theirs], dst_ref=acc_in, send_sem=one_s.at[1], recv_sem=one_r.at[1],
        device_id=(sibling, band), device_id_type=MESH)
    acc_copy.start()
    acc_copy.wait_recv()
    packed[0] = acc[:, mine] + acc_in[...]

    def place_of(t):
        return 2 * t - 1 if 0 < t <= half else 2 * ((n - t) % n)

    def gather_copy(t):
        return pltpu.make_async_remote_copy(
            src_ref=packed.at[0], dst_ref=packed.at[place_of(t)], send_sem=gat_s.at[t - 1], recv_sem=gat_r.at[t - 1],
            device_id=(member(t), band), device_id_type=MESH)

    order = sorted(range(1, n), key=lambda t: -min(t, n - t))
    for t in order:
        gather_copy(t).start()
    place(n - 2)
    place(n - 1)

    column = lax.broadcasted_iota(jnp.int32, (width, wide), 1) + ka * columns
    block = functions // blocks
    masks = []
    for f in range(cells):
        mask = jnp.zeros((width, wide), f32)
        for i in range(blocks):
            keep = (column >= i * block) & (column < (i + 1) * block)
            mask = jnp.where(keep, pattern[f, i].astype(f32), mask)
        masks.append(mask)

    @pl.loop(1, half + 1)
    def _(s):
        for h in range(CHUNKS):
            for side in (True, False):
                @pl.when(s <= steps(side, h))
                def _():
                    ring_copy(side, s, h).wait_send()

    @pl.loop(0, n)
    def _(t):
        for g in range(1, bands):
            window_copy(g, t).wait_send()

    acc_copy.wait_send()
    for t in order:
        gather_copy(t).wait_recv()

    rotated = lax.broadcasted_iota(jnp.int32, (rows, lanes), 1)
    flip = jnp.where(rotated < lanes // 2, -1.0, 1.0)
    real = [packed[t] for t in range(n)]
    left = jnp.concatenate(
        [jnp.concatenate(real, 1), jnp.concatenate([flip * swap(x) for x in real], 1)], 0)
    high = left.astype(bf16)
    low = (left - high.astype(f32)).astype(bf16)
    factors = jnp.concatenate([high, low], 0)

    def part_of(c):
        value = dot(factors, stack[c].reshape(n * lanes, wide))
        return value[:2 * rows] + value[2 * rows:]

    part[...] = part_of(0)
    part_copy = pltpu.make_async_remote_copy(
        src_ref=part, dst_ref=part_in, send_sem=one_s.at[2], recv_sem=one_r.at[2],
        device_id=(sibling, band), device_id_type=MESH)
    part_copy.start()
    kept = part_of(1)
    part_copy.wait_recv()
    whole = kept + part_in[...]
    for ri in range(2):
        for f in range(cells):
            spot = (ri * cells + f) * width
            out[f, ri] = (whole[spot:spot + width] * masks[f])[:, :columns]

    for t in order:
        gather_copy(t).wait_send()
    part_copy.wait_send()


def solution(mesh):
    nk, bands = mesh.shape["ka"], mesh.shape["band"]
    n = nk // 2

    def shards(coefficients, class_weight, diff_class, frag_cells, block_pattern):
        occupied, functions = coefficients.shape[2:]
        width = occupied // bands
        cells, blocks = block_pattern.shape
        padded = (functions + LANES - 1) // LANES * LANES
        columns = functions // nk
        window = (2 * columns + 2 * LANES - 2) // LANES * LANES
        wide = (columns + LANES - 1) // LANES * LANES
        lanes = 2 * bands * STRIDE
        rows = cells * width
        hbm = pl.BlockSpec(memory_space=pltpu.HBM)
        bf16, f32 = jnp.bfloat16, jnp.float32
        dma = pltpu.SemaphoreType.DMA
        operands = (coefficients, class_weight, diff_class, frag_cells, block_pattern)
        return pl.pallas_call(
            functools.partial(kernel, nk, bands, width, occupied, functions, blocks, cells),
            out_shape=jax.ShapeDtypeStruct((cells, 2, width, columns), f32),
            in_specs=[hbm] * 5,
            out_specs=pl.BlockSpec(memory_space=pltpu.VMEM),
            scratch_shapes=[
                pltpu.VMEM(coefficients.shape, bf16),
                *[pltpu.SMEM(x.shape, x.dtype) for x in operands[1:]],
                pltpu.VMEM((padded, 2 * lanes), bf16),
                pltpu.VMEM((n, 2 * width, padded), bf16),
                pltpu.VMEM((bands - 1, n, 2 * width, window), bf16),
                pltpu.VMEM((2, n, lanes, wide), bf16),
                pltpu.VMEM((2 * cells, n, 2 * lanes), f32),
                pltpu.VMEM((rows, 2 * lanes), f32),
                pltpu.VMEM((rows, lanes), f32),
                pltpu.VMEM((n, rows, lanes), f32),
                pltpu.VMEM((2 * rows, wide), f32),
                pltpu.VMEM((2 * rows, wide), f32),
                dma((5,)),
                *[dma((n // 2, CHUNKS))] * 4,
                dma((bands - 1, n)), dma((bands - 1, n)),
                dma((n - 1,)), dma((n - 1,)), dma((3,)), dma((3,)),
            ],
            compiler_params=pltpu.CompilerParams(
                collective_id=0, has_side_effects=True, vmem_limit_bytes=63 * 2**20),
            cost_estimate=pl.CostEstimate(
                flops=8 * n * width * lanes * padded, bytes_accessed=8 * n * width * padded, transcendentals=0),
            name="exchange",
        )(*operands)

    placed = (P("ka", None, None, None), P(), P(), P(), P())
    return jax.shard_map(
        shards, mesh=mesh, in_specs=placed, out_specs=P(None, None, "band", "ka"), check_vma=False)
```
